32 devices in a mesh: groups: 2 (over y), expert: 4 (over z), dp: 4 (over x, core).
Axes of the slice: x: 2, y: 2, z: 4, core: 2. Of those that a mesh axis runs over, the one named last changes fastest.
Arguments:
- tokens: bfloat16 [4096, 2048], P(('groups', 'expert', 'dp')), parts along dimension 0, may hold values from -6 to 6
- cotangent: bfloat16 [4096, 2048], P(('groups', 'expert', 'dp')), parts along dimension 0, may hold values from -6 to 6
- expert_ids: int32 [4096, 2], P(('groups', 'expert', 'dp')), parts along dimension 0, may hold values from 0 to 3, as said below
- gate_fix: int32 [4096, 2], P(('groups', 'expert', 'dp')), parts along dimension 0, may hold values from 4096 to 65535
- w_up: bfloat16 [4, 2048, 768], P('expert', 'dp'), may hold values from -0.125 to 0.125
- w_down: bfloat16 [4, 768, 2048], P('expert', None, 'dp'), may hold values from -0.21875 to 0.21875
Outputs:
- mixed: bfloat16 [4096, 2048], P(('groups', 'expert', 'dp')), parts along dimension 0
- grad_tokens: bfloat16 [4096, 2048], P(('groups', 'expert', 'dp')), parts along dimension 0
- grad_up: bfloat16 [8, 2048, 768], P(('groups', 'expert'), 'dp'), parts along dimension 0
- grad_down: bfloat16 [8, 768, 2048], P(('groups', 'expert'), None, 'dp'), parts along dimension 0
The draws below stay inside these ranges and needn't reach their ends.
There are 2 independent parts, one for each index of `groups`. The reference program is written for one: setup_inputs(seed, part) draws one part's arguments, and reference() takes and returns one part's arrays. A program takes and returns all parts, laid end to end along the dimension named above; an argument that names none is the same for every part. Nothing has to cross between parts.
Inputs may be any that keep to these rules, and one draw needn't show every extreme that they name: `expert_ids`: column 0 of row t is its home expert t // (128 * 4); column 1 is the next or the previous expert on the cycle of 4. Among the 128 rows of one device at most 80 name the next expert and at most 80 name the previous one; both bounds are reached by some device in every draw.
All inputs are finite; a program needn't handle non-finite values.
Results may differ from the reference program's by a relative error of at most 0.0065.
Values may be sent and summed in bfloat16 or wider, within the bound.
A program may use at most 64 MiB of HBM per device.

```python
import jax
import jax.numpy as jnp
from jax import lax

D = 2048
FF = 768
TOK_DEV = 128
CAP = 80
EXPERTS = 4
TOKENS = 2048
N_EXPERT = 4
N_DP = 4


def draw_expert_ids(key, part):
    key = jax.random.fold_in(key, 11)
    first, second, third, fourth = jax.random.split(key, 4)
    blocks = TOKENS // TOK_DEV
    lowest = TOK_DEV - CAP
    counts = jax.random.randint(first, (blocks,), lowest, CAP + 1)
    full_next = jax.random.randint(second, (), 0, blocks)
    full_prev = (full_next + 1 + jax.random.randint(third, (), 0, blocks - 1)) % blocks
    places = jnp.arange(blocks, dtype=jnp.int32)
    counts = jnp.where(places == full_prev, lowest, counts)
    counts = jnp.where(places == full_next, CAP, counts)
    orders = jax.vmap(lambda one_key: jax.random.permutation(one_key, TOK_DEV))(jax.random.split(fourth, blocks))
    goes_next = orders < counts[:, None]
    home = (places // N_DP)[:, None] + jnp.zeros((blocks, TOK_DEV), jnp.int32)
    side = jnp.where(goes_next, (home + 1) % N_EXPERT, (home - 1 + N_EXPERT) % N_EXPERT)
    return jnp.stack([home, side], axis=-1).reshape(TOKENS, 2).astype(jnp.int32)


def set_ends(drawn, own_key, low, largest):
    extent = drawn.shape
    place = [jax.random.randint(jax.random.fold_in(own_key, axis), (), 0, extent[axis]) for axis in range(len(extent))]
    drawn = drawn.at[tuple(place)].set(low)
    longest = extent.index(max(extent))
    place[longest] = (place[longest] + 1) % extent[longest]
    return drawn.at[tuple(place)].set(largest)


def steps_of(own_key, dims, pieces, smallest, high):
    level = 1.0
    for dim, blocks in pieces:
        heights = jax.random.uniform(jax.random.fold_in(jax.random.fold_in(own_key, 6), dim), (blocks,), jnp.float32, smallest / len(pieces), high / len(pieces))
        level = level * jnp.repeat(jnp.exp(heights), dims[dim] // blocks).reshape((-1,) + (1,) * (len(dims) - 1 - dim))
    return level


def centred(stream_key, dims, width, reach, pieces=(), kind=jnp.bfloat16):
    result = width * jax.random.normal(stream_key, dims, jnp.float32)
    if pieces:
        result = result * steps_of(stream_key, dims, pieces, -0.22, 0.18)
    return jnp.clip(result, -reach, reach).astype(kind)


def setup_inputs(seed: int = 0, part: int = 0) -> dict:
    key_list = jax.random.split(jax.random.key(seed), 7)
    part_keys = jax.random.split(jax.random.fold_in(key_list[6], part), 7)
    return {
        "tokens": centred(part_keys[0], (TOKENS, D), 1.0, 6.0, ((0, 16),)),
        "cotangent": centred(part_keys[1], (TOKENS, D), 1.0, 6.0, ((0, 16),)),
        "expert_ids": draw_expert_ids(jax.random.fold_in(jax.random.fold_in(key_list[6], part), 71), part),
        "gate_fix": set_ends(jax.random.randint(part_keys[3], (TOKENS, 2), 4096, 65536), jax.random.fold_in(part_keys[3], 1), 4096, 65535).astype(jnp.int32),
        "w_up": centred(key_list[4], (EXPERTS, D, FF), D ** -0.5, 0.125, ((0, 4), (1, 4))),
        "w_down": centred(key_list[5], (EXPERTS, FF, D), FF ** -0.5, 0.21875, ((0, 4), (2, 4))),
    }


def sigmoid_of(value):
    return 1.0 / (1.0 + jnp.exp(-value))


def reference(tokens, cotangent, expert_ids, gate_fix, w_up, w_down):
    cycle = N_EXPERT
    slots = N_DP
    flat_rows = slots * TOK_DEV
    tok = tokens.reshape(cycle, slots, TOK_DEV, D)
    cot = cotangent.reshape(cycle, slots, TOK_DEV, D)
    ids = expert_ids.reshape(cycle, slots, TOK_DEV, 2)
    fixed = gate_fix.astype(jnp.float32).reshape(cycle, slots, TOK_DEV, 2)
    gates = fixed / jnp.sum(fixed, axis=-1, keepdims=True)

    def one_expert(carry, expert):
        mix_acc, grad_acc = carry
        up_mat = w_up[expert]
        down_mat = w_down[expert]
        up_sum = jnp.zeros((slots, D, FF), jnp.float32)
        down_sum = jnp.zeros((slots, FF, D), jnp.float32)
        for offset in range(3):
            source = ((expert + offset - 1 + cycle) % cycle).astype(jnp.int32)
            rows_in = tok[source]
            weight = jnp.sum(jnp.where(ids[source] == expert, gates[source], jnp.float32(0.0)), axis=-1)
            scaled = (weight[..., None] * cot[source].astype(jnp.float32)).astype(jnp.bfloat16)
            flat_in = rows_in.reshape(flat_rows, D)
            flat_scaled = scaled.reshape(flat_rows, D)
            hidden = jnp.dot(flat_in, up_mat, preferred_element_type=jnp.float32)
            sig = sigmoid_of(hidden)
            act = (hidden * sig).astype(jnp.bfloat16)
            expert_out = jnp.dot(act, down_mat, preferred_element_type=jnp.float32).astype(jnp.bfloat16)
            d_act = lax.dot_general(flat_scaled, down_mat, (((1,), (1,)), ((), ())), preferred_element_type=jnp.float32)
            d_hidden = (d_act * sig * (1.0 + hidden * (1.0 - sig))).astype(jnp.bfloat16)
            d_in = lax.dot_general(d_hidden, up_mat, (((1,), (1,)), ((), ())), preferred_element_type=jnp.float32).astype(jnp.bfloat16)
            contrib = weight[..., None] * expert_out.astype(jnp.float32).reshape(slots, TOK_DEV, D)
            mix_acc = mix_acc.at[source].add(contrib)
            grad_acc = grad_acc.at[source].add(d_in.astype(jnp.float32).reshape(slots, TOK_DEV, D))
            up_sum = up_sum + jnp.einsum("ptd,ptf->pdf", rows_in.astype(jnp.float32), d_hidden.reshape(slots, TOK_DEV, FF).astype(jnp.float32))
            down_sum = down_sum + jnp.einsum("ptf,ptd->pfd", act.reshape(slots, TOK_DEV, FF).astype(jnp.float32), scaled.astype(jnp.float32))
        up_round = lax.optimization_barrier(up_sum.astype(jnp.bfloat16)).astype(jnp.float32)
        down_round = lax.optimization_barrier(down_sum.astype(jnp.bfloat16)).astype(jnp.float32)
        grad_up_e = jnp.sum(up_round, axis=0).astype(jnp.bfloat16)
        grad_down_e = jnp.sum(down_round, axis=0).astype(jnp.bfloat16)
        return (mix_acc, grad_acc), (grad_up_e, grad_down_e)

    start = (jnp.zeros((cycle, slots, TOK_DEV, D), jnp.float32), jnp.zeros((cycle, slots, TOK_DEV, D), jnp.float32))
    (mix_acc, grad_acc), (grad_up, grad_down) = lax.scan(one_expert, start, jnp.arange(cycle, dtype=jnp.int32))
    mixed = mix_acc.reshape(TOKENS, D).astype(jnp.bfloat16)
    grad_tokens = grad_acc.reshape(TOKENS, D).astype(jnp.bfloat16)
    return (mixed, grad_tokens, grad_up, grad_down)
```

```python
import functools

import jax
import jax.numpy as jnp
from jax import lax
from jax.experimental import pallas as pl
from jax.experimental.pallas import tpu as pltpu
from jax.sharding import PartitionSpec as P

CAP = 80
MESH = pl.DeviceIdType.MESH
F32 = jnp.float32
BF16 = jnp.bfloat16


def nt_dot(left, right):
    return lax.dot_general(left, right, (((1,), (1,)), ((), ())), preferred_element_type=F32)


def tn_dot(left, right):
    return lax.dot_general(left, right, (((0,), (0,)), ((), ())), preferred_element_type=F32)


def dot(left, right):
    return jnp.dot(left, right, preferred_element_type=F32)


def remote(src, dst, sends, recvs, where, device):
    return pltpu.make_async_remote_copy(
        src_ref=src,
        dst_ref=dst,
        send_sem=sends.at[where],
        recv_sem=recvs.at[where],
        device_id=device,
        device_id_type=MESH,
    )


def silu_parts(hidden, d_act):
    sig = 1.0 / (1.0 + jnp.exp(-hidden))
    act = (hidden * sig).astype(BF16)
    d_hidden = (d_act * sig * (1.0 + hidden * (1.0 - sig))).astype(BF16)
    return act, d_hidden


def kernel(
    groups, cycle, slots,
    tok, cot, ids, fix, up_in, down_in,
    mixed, grad_tok, grad_up, grad_down,
    up_w, down_w, pick, home_scl, snd_tok, snd_scl, vis_tok, vis_scl,
    acc_h, acc_d, acc_hv, acc_dv, act_h, dh_h, act_v, dh_v, out_h, din_h,
    ret_out, ret_din, back_out, back_din,
    up_pair, down_pair, up_pair_in, down_pair_in, up_own, down_own,
    up_x, down_x, up_x_in, down_x_in,
    local_sem, pair_s, pair_r, x_s, x_r, y_s, y_r, f_s, f_r, d_s, d_r, r_s, r_r,
    gp_s, gp_r, gx_s, gx_r,
):
    rows = tok.shape[0]
    width = tok.shape[1]
    part = width // slots
    highs = slots // 2
    group = lax.axis_index("groups")
    place = lax.axis_index("expert")
    me = lax.axis_index("dp")
    high = me // 2
    low = me % 2
    other = 1 - low
    pair = high * 2 + other
    after = lax.rem(place + 1, cycle)
    before = lax.rem(place + cycle - 1, cycle)

    def columns(block):
        return pl.ds(pl.multiple_of(block * part, part), part)

    barrier = pltpu.get_barrier_semaphore()
    peers = [{"dp": pair}, {"expert": after}, {"expert": before}]
    peers += [{"dp": lax.rem(high + k, highs) * 2 + low} for k in range(1, highs)]
    peers += [{"groups": lax.rem(group + q, groups)} for q in range(1, groups)]
    for peer in peers:
        pl.semaphore_signal(barrier, inc=1, device_id=peer, device_id_type=MESH)

    goes = jnp.where(ids[:, 1:2] == after, 1.0, 0.0).astype(F32)
    lane = lax.broadcasted_iota(jnp.int32, (rows, rows), 1)
    line = lax.broadcasted_iota(jnp.int32, (rows, rows), 0)
    flags = jnp.where(lane == 0, goes, 1.0 - goes).astype(BF16)
    counts = tn_dot(flags, jnp.where(line <= lane, 1.0, 0.0).astype(BF16))
    marks = tn_dot(flags, jnp.where(line == lane, 1.0, 0.0).astype(BF16))
    slot = lax.broadcasted_iota(jnp.int32, (2 * CAP, rows), 0)
    first = slot < CAP
    wanted = jnp.where(first, slot, slot - CAP).astype(F32) + 1.0
    count = jnp.where(first, counts[0:1, :], counts[1:2, :])
    mark = jnp.where(first, marks[0:1, :], marks[1:2, :])
    pick[...] = jnp.where(count == wanted, mark, 0.0).astype(BF16)
    fixed = fix[...].astype(F32)
    total = fixed[:, 0:1] + fixed[:, 1:2]
    home_gate = fixed[:, 0:1] / total
    side_gate = fixed[:, 1:2] / total

    pl.semaphore_wait(barrier, len(peers))

    weights = ((up_in, up_w), (down_in, down_w))
    local_copies = []
    sends = []
    pair_copies = []
    x_copies = [[], []]
    for w, (own, full) in enumerate(weights):
        half = own.shape[1] // groups
        mine = pl.ds(pl.multiple_of(group * half, half), half)
        for k in range(1, highs):
            copy = remote(
                own.at[0, mine], full.at[me, mine], x_s, x_r, (w, k - 1),
                {"dp": lax.rem(high + k, highs) * 2 + low},
            )
            copy.start()
            x_copies[w].append(copy)
            sends.append(copy)
        copy = remote(own.at[0], full.at[me], pair_s, pair_r, w, {"dp": pair})
        copy.start()
        pair_copies.append(copy)
        sends.append(copy)
        copy = pltpu.make_async_copy(own.at[0], full.at[me], local_sem.at[w])
        copy.start()
        local_copies.append(copy)

    picked = pick[...]
    d_copies = []

    def dispatch(array, src, dst):
        for way, target in enumerate((after, before)):
            span = pl.ds(way * CAP, CAP)
            copy = remote(src.at[span], dst.at[span], d_s, d_r, (array, way), {"expert": target})
            copy.start()
            d_copies.append(copy)
            sends.append(copy)

    snd_tok[...] = dot(picked, tok[...]).astype(BF16)
    dispatch(0, snd_tok, vis_tok)
    wide = cot[...].astype(F32)
    snd_scl[...] = dot(picked, (side_gate * wide).astype(BF16)).astype(BF16)
    dispatch(1, snd_scl, vis_scl)
    home_scl[...] = (home_gate * wide).astype(BF16)

    def add_up(block, first_one, src, acc):
        term = dot(src[:, columns(block)], up_w[block])
        acc[...] = term if first_one else acc[...] + term

    def add_down(block, first_one, src, acc):
        term = nt_dot(src[:, columns(block)], down_w[block])
        acc[...] = term if first_one else acc[...] + term

    adders = ((add_up, tok, acc_h), (add_down, home_scl, acc_d))

    for w, (add, src, acc) in enumerate(adders):
        local_copies[w].wait()
        add(me, True, src, acc)
    for w, (add, src, acc) in enumerate(adders):
        pair_copies[w].wait_recv()
        add(pair, False, src, acc)

    y_copies = {}
    f_copies = {}
    for k in range(1, highs):
        came = lax.rem(high + highs - k, highs) * 2 + low
        for w, (own, full) in enumerate(weights):
            half = own.shape[1] // groups
            mine = pl.ds(pl.multiple_of(group * half, half), half)
            x_copies[w][k - 1].wait_recv()
            piece = full.at[came, mine]
            for q in range(1, groups):
                copy = remote(
                    piece, piece, y_s, y_r, (w, k - 1, q - 1), {"groups": lax.rem(group + q, groups)}
                )
                copy.start()
                y_copies[w, k, q] = copy
                sends.append(copy)
            copy = remote(piece, piece, f_s, f_r, (w, k - 1, 0), {"dp": pair})
            copy.start()
            f_copies[w, k, 0] = copy
            sends.append(copy)
    for k in range(1, highs):
        came = lax.rem(high + highs - k, highs) * 2 + low
        for w, (own, full) in enumerate(weights):
            half = own.shape[1] // groups
            for q in range(1, groups):
                y_copies[w, k, q].wait_recv()
                theirs = lax.rem(group + groups - q, groups)
                piece = full.at[came, pl.ds(pl.multiple_of(theirs * half, half), half)]
                copy = remote(piece, piece, f_s, f_r, (w, k - 1, q), {"dp": pair})
                copy.start()
                f_copies[w, k, q] = copy
                sends.append(copy)
            add, src, acc = adders[w]
            add(came, False, src, acc)
    for k in range(1, highs):
        came = lax.rem(high + highs - k, highs) * 2 + other
        for w in range(2):
            for q in range(groups):
                f_copies[w, k, q].wait_recv()
            add, src, acc = adders[w]
            add(came, False, src, acc)

    act, d_hidden = silu_parts(acc_h[...], acc_d[...])
    act_h[...] = act
    dh_h[...] = d_hidden

    def home_block(block, carry):
        span = columns(block)
        out_h[:, span] = dot(act_h[...], down_w[block]).astype(BF16)
        din_h[:, span] = nt_dot(dh_h[...], up_w[block]).astype(BF16)
        return carry

    lax.fori_loop(0, slots, home_block, 0)

    for copy in d_copies:
        copy.wait_recv()

    acc_hv[...] = dot(vis_tok[:, 0:part], up_w[0])
    acc_dv[...] = nt_dot(vis_scl[:, 0:part], down_w[0])

    def visit_block(block, carry):
        add_up(block, False, vis_tok, acc_hv)
        add_down(block, False, vis_scl, acc_dv)
        return carry

    lax.fori_loop(1, slots, visit_block, 0)
    act, d_hidden = silu_parts(acc_hv[...], acc_dv[...])
    act_v[...] = act
    dh_v[...] = d_hidden

    r_copies = []

    def returns(array):
        for block in range(slots):
            span = pl.ds(block * part, part)
            if array == 0:
                src, dst = ret_out, back_out
                src[:, span] = dot(act_v[...], down_w[block]).astype(BF16)
            else:
                src, dst = ret_din, back_din
                src[:, span] = nt_dot(dh_v[...], up_w[block]).astype(BF16)
            for way, target in enumerate((before, after)):
                lines = pl.ds(way * CAP, CAP)
                copy = remote(
                    src.at[lines, span], dst.at[lines, span], r_s, r_r, (array, block, way),
                    {"expert": target},
                )
                copy.start()
                r_copies.append(copy)
                sends.append(copy)

    hidden_width = act_h.shape[1]

    def up_term(block, dst):
        step = min(256, part)

        def one(i, carry):
            span = pl.ds(pl.multiple_of(block * part + i * step, step), step)
            term = tn_dot(tok[:, span], dh_h[...]) + tn_dot(vis_tok[:, span], dh_v[...])
            dst[pl.ds(pl.multiple_of(i * step, step), step), :] = term.astype(dst.dtype)
            return carry

        lax.fori_loop(0, part // step, one, 0)

    def down_term(block, dst):
        step = 256
        span = columns(block)

        def one(i, carry):
            lines = pl.ds(pl.multiple_of(i * step, step), step)
            term = tn_dot(act_h[:, lines], home_scl[:, span]) + tn_dot(act_v[:, lines], vis_scl[:, span])
            dst[lines, :] = term.astype(dst.dtype)
            return carry

        lax.fori_loop(0, hidden_width // step, one, 0)

    terms = (
        (up_term, up_pair, up_pair_in, up_own, up_x, up_x_in, grad_up),
        (down_term, down_pair, down_pair_in, down_own, down_x, down_x_in, grad_down),
    )
    gp_copies = {}
    gx_copies = {}

    def make_terms(w, k):
        make, pair_out, pair_in, own = terms[w][:4]
        target = lax.rem(high + k, highs) * 2
        make(target + other, pair_out.at[k])
        copy = remote(pair_out.at[k], pair_in.at[k], gp_s, gp_r, (w, k), {"dp": pair})
        copy.start()
        gp_copies[w, k] = copy
        sends.append(copy)
        make(target + low, own.at[k])

    def send_x(w, k):
        pair_in, own, out, into = terms[w][2:6]
        gp_copies[w, k].wait_recv()
        out[k - 1] = (own[k] + pair_in[k].astype(F32)).astype(BF16)
        copy = remote(
            out.at[k - 1], into.at[k - 1], gx_s, gx_r, (w, k - 1),
            {"dp": lax.rem(high + k, highs) * 2 + low},
        )
        copy.start()
        gx_copies[w, k] = copy
        sends.append(copy)

    for k in range(1, highs):
        make_terms(0, k)
    returns(0)
    for k in range(1, highs):
        send_x(0, k)
    for k in range(1, highs):
        make_terms(1, k)
    returns(1)
    for k in range(1, highs):
        send_x(1, k)
    for w in range(2):
        make_terms(w, 0)
    for w in range(2):
        pair_in, own = terms[w][2:4]
        gp_copies[w, 0].wait_recv()
        own[0] = own[0] + pair_in[0].astype(F32)

    for copy in r_copies:
        copy.wait_recv()
    picked = pick[...]
    side = tn_dot(picked, back_out[...])
    mixed[...] = (home_gate * out_h[...].astype(F32) + side_gate * side).astype(BF16)
    side = tn_dot(picked, back_din[...])
    grad_tok[...] = (din_h[...].astype(F32) + side).astype(BF16)

    for w in range(2):
        own, _, into, result = terms[w][3:7]
        whole = own[0]
        for k in range(1, highs):
            gx_copies[w, k].wait_recv()
            whole = whole + into[k - 1].astype(F32)
        result[0] = whole.astype(BF16)
    for copy in sends:
        copy.wait_send()


def local(tokens, cotangent, expert_ids, gate_fix, w_up, w_down):
    rows, width = tokens.shape
    groups = lax.axis_size("groups")
    cycle = lax.axis_size("expert")
    slots = lax.axis_size("dp")
    highs = slots // 2
    hidden = w_up.shape[2]
    part = width // slots
    side = 2 * CAP
    vmem = pl.BlockSpec(memory_space=pltpu.VMEM)
    anywhere = pl.BlockSpec(memory_space=pl.ANY)
    dma = pltpu.SemaphoreType.DMA
    far = highs - 1
    return pl.pallas_call(
        functools.partial(kernel, groups, cycle, slots),
        out_shape=(
            jax.ShapeDtypeStruct((rows, width), BF16),
            jax.ShapeDtypeStruct((rows, width), BF16),
            jax.ShapeDtypeStruct((1, part, hidden), BF16),
            jax.ShapeDtypeStruct((1, hidden, part), BF16),
        ),
        in_specs=[vmem] * 4 + [anywhere] * 2,
        out_specs=[vmem] * 4,
        scratch_shapes=[
            pltpu.VMEM((slots, part, hidden), BF16),
            pltpu.VMEM((slots, hidden, part), BF16),
            pltpu.VMEM((side, rows), BF16),
            pltpu.VMEM((rows, width), BF16),
            pltpu.VMEM((side, width), BF16),
            pltpu.VMEM((side, width), BF16),
            pltpu.VMEM((side, width), BF16),
            pltpu.VMEM((side, width), BF16),
            pltpu.VMEM((rows, hidden), F32),
            pltpu.VMEM((rows, hidden), F32),
            pltpu.VMEM((side, hidden), F32),
            pltpu.VMEM((side, hidden), F32),
            pltpu.VMEM((rows, hidden), BF16),
            pltpu.VMEM((rows, hidden), BF16),
            pltpu.VMEM((side, hidden), BF16),
            pltpu.VMEM((side, hidden), BF16),
            pltpu.VMEM((rows, width), BF16),
            pltpu.VMEM((rows, width), BF16),
            pltpu.VMEM((side, width), BF16),
            pltpu.VMEM((side, width), BF16),
            pltpu.VMEM((side, width), BF16),
            pltpu.VMEM((side, width), BF16),
            pltpu.VMEM((highs, part, hidden), BF16),
            pltpu.VMEM((highs, hidden, part), BF16),
            pltpu.VMEM((highs, part, hidden), BF16),
            pltpu.VMEM((highs, hidden, part), BF16),
            pltpu.VMEM((highs, part, hidden), F32),
            pltpu.VMEM((highs, hidden, part), F32),
            pltpu.VMEM((far, part, hidden), BF16),
            pltpu.VMEM((far, hidden, part), BF16),
            pltpu.VMEM((far, part, hidden), BF16),
            pltpu.VMEM((far, hidden, part), BF16),
            dma((2,)),
            dma((2,)),
            dma((2,)),
            dma((2, far)),
            dma((2, far)),
            dma((2, far, groups - 1)),
            dma((2, far, groups - 1)),
            dma((2, far, groups)),
            dma((2, far, groups)),
            dma((2, 2)),
            dma((2, 2)),
            dma((2, slots, 2)),
            dma((2, slots, 2)),
            dma((2, highs)),
            dma((2, highs)),
            dma((2, far)),
            dma((2, far)),
        ],
        compiler_params=pltpu.CompilerParams(
            collective_id=0, has_side_effects=True, vmem_limit_bytes=56 * 1024 * 1024
        ),
    )(tokens, cotangent, expert_ids, gate_fix, w_up, w_down)


def solution(mesh):
    in_specs = (
        P(("groups", "expert", "dp"), None),
        P(("groups", "expert", "dp"), None),
        P(("groups", "expert", "dp"), None),
        P(("groups", "expert", "dp"), None),
        P("expert", "dp", None),
        P("expert", None, "dp"),
    )
    out_specs = (
        P(("groups", "expert", "dp"), None),
        P(("groups", "expert", "dp"), None),
        P(("groups", "expert"), "dp", None),
        P(("groups", "expert"), None, "dp"),
    )
    return jax.shard_map(local, mesh=mesh, in_specs=in_specs, out_specs=out_specs, check_vma=False)
```

```python
import functools

import jax
import jax.numpy as jnp
from jax import lax
from jax.experimental import pallas as pl
from jax.experimental.pallas import tpu as pltpu
from jax.sharding import PartitionSpec as P

CAP = 80
MESH = pl.DeviceIdType.MESH
F32 = jnp.float32
BF16 = jnp.bfloat16


def nt_dot(left, right):
    return lax.dot_general(left, right, (((1,), (1,)), ((), ())), preferred_element_type=F32)


def tn_dot(left, right):
    return lax.dot_general(left, right, (((0,), (0,)), ((), ())), preferred_element_type=F32)


def dot(left, right):
    return jnp.dot(left, right, preferred_element_type=F32)


def remote(src, dst, sends, recvs, where, device):
    return pltpu.make_async_remote_copy(
        src_ref=src,
        dst_ref=dst,
        send_sem=sends.at[where],
        recv_sem=recvs.at[where],
        device_id=device,
        device_id_type=MESH,
    )


def silu_parts(hidden, d_act):
    sig = 1.0 / (1.0 + jnp.exp(-hidden))
    act = (hidden * sig).astype(BF16)
    d_hidden = (d_act * sig * (1.0 + hidden * (1.0 - sig))).astype(BF16)
    return act, d_hidden


def kernel(
    groups, cycle, slots,
    tok, cot, ids, fix, up_in, down_in,
    mixed_out, grad_tok_out, grad_up_out, grad_down_out,
    mixed, grad_tok, grad_up, grad_down, out_sem,
    up_w, down_w, pick, home_scl, snd_tok, snd_scl, vis_tok, vis_scl,
    acc_h, acc_d, acc_hv, acc_dv, act_h, dh_h, act_v, dh_v, out_h, din_h,
    ret_out, ret_din, back_out, back_din,
    up_pair, down_pair, up_pair_in, down_pair_in, up_own, down_own,
    up_x, down_x, up_x_in, down_x_in,
    local_sem, pair_s, pair_r, x_s, x_r, y_s, y_r, f_s, f_r, d_s, d_r, r_s, r_r,
    gp_s, gp_r, gx_s, gx_r,
):
    rows = tok.shape[0]
    width = tok.shape[1]
    part = width // slots
    highs = slots // 2
    group = lax.axis_index("groups")
    place = lax.axis_index("expert")
    me = lax.axis_index("dp")
    high = me // 2
    low = me % 2
    other = 1 - low
    pair = high * 2 + other
    after = lax.rem(place + 1, cycle)
    before = lax.rem(place + cycle - 1, cycle)

    def columns(block):
        return pl.ds(pl.multiple_of(block * part, part), part)

    barrier = pltpu.get_barrier_semaphore()
    peers = [{"dp": pair}, {"expert": after}, {"expert": before}]
    peers += [{"dp": lax.rem(high + k, highs) * 2 + low} for k in range(1, highs)]
    peers += [{"groups": lax.rem(group + q, groups)} for q in range(1, groups)]
    for peer in peers:
        pl.semaphore_signal(barrier, inc=1, device_id=peer, device_id_type=MESH)

    lane = lax.broadcasted_iota(jnp.int32, (rows, rows), 1)
    line = lax.broadcasted_iota(jnp.int32, (rows, rows), 0)
    eye = jnp.where(line == lane, 1.0, 0.0).astype(BF16)
    goes = jnp.where(ids[1:2, :] == after, 1.0, 0.0).astype(F32)
    upper = lax.broadcasted_iota(jnp.int32, (8, rows), 0) == 0
    marks = jnp.where(upper, goes, 1.0 - goes)
    counts = dot(marks.astype(BF16), jnp.where(line <= lane, 1.0, 0.0).astype(BF16))
    slot = lax.broadcasted_iota(jnp.int32, (2 * CAP, rows), 0)
    first = slot < CAP
    wanted = jnp.where(first, slot, slot - CAP).astype(F32) + 1.0
    count = jnp.where(first, counts[0:1, :], counts[1:2, :])
    mark = jnp.where(first, marks[0:1, :], marks[1:2, :])
    pick[...] = jnp.where(count == wanted, mark, 0.0).astype(BF16)
    fixed = fix[...]
    split = jnp.concatenate([fixed // 256, fixed % 256], axis=0).astype(F32).astype(BF16)
    turned = nt_dot(eye, split)
    home_fix = turned[:, 0:1] * 256.0 + turned[:, 2:3]
    side_fix = turned[:, 1:2] * 256.0 + turned[:, 3:4]
    total = home_fix + side_fix
    home_gate = home_fix / total
    side_gate = side_fix / total

    pl.semaphore_wait(barrier, len(peers))

    weights = ((up_in, up_w), (down_in, down_w))
    local_copies = []
    sends = []
    pair_copies = []
    x_copies = [[], []]
    for w, (own, full) in enumerate(weights):
        half = own.shape[1] // groups
        mine = pl.ds(pl.multiple_of(group * half, half), half)
        for k in range(1, highs):
            copy = remote(
                own.at[0, mine], full.at[me, mine], x_s, x_r, (w, k - 1),
                {"dp": lax.rem(high + k, highs) * 2 + low},
            )
            copy.start()
            x_copies[w].append(copy)
            sends.append(copy)
        copy = remote(own.at[0], full.at[me], pair_s, pair_r, w, {"dp": pair})
        copy.start()
        pair_copies.append(copy)
        sends.append(copy)
        copy = pltpu.make_async_copy(own.at[0], full.at[me], local_sem.at[w])
        copy.start()
        local_copies.append(copy)

    picked = pick[...]
    d_copies = []

    def dispatch(array, src, dst):
        for way, target in enumerate((after, before)):
            span = pl.ds(way * CAP, CAP)
            copy = remote(src.at[span], dst.at[span], d_s, d_r, (array, way), {"expert": target})
            copy.start()
            d_copies.append(copy)
            sends.append(copy)

    snd_tok[...] = dot(picked, tok[...]).astype(BF16)
    dispatch(0, snd_tok, vis_tok)
    wide = cot[...].astype(F32)
    snd_scl[...] = dot(picked, (side_gate * wide).astype(BF16)).astype(BF16)
    dispatch(1, snd_scl, vis_scl)
    home_scl[...] = (home_gate * wide).astype(BF16)

    def add_up(block, first_one, src, acc):
        term = dot(src[:, columns(block)], up_w[block])
        acc[...] = term if first_one else acc[...] + term

    def add_down(block, first_one, src, acc):
        term = nt_dot(src[:, columns(block)], down_w[block])
        acc[...] = term if first_one else acc[...] + term

    adders = ((add_up, tok, acc_h), (add_down, home_scl, acc_d))

    for w, (add, src, acc) in enumerate(adders):
        local_copies[w].wait()
        add(me, True, src, acc)
    for w, (add, src, acc) in enumerate(adders):
        pair_copies[w].wait_recv()
        add(pair, False, src, acc)

    y_copies = {}
    f_copies = {}
    for k in range(1, highs):
        came = lax.rem(high + highs - k, highs) * 2 + low
        for w, (own, full) in enumerate(weights):
            half = own.shape[1] // groups
            mine = pl.ds(pl.multiple_of(group * half, half), half)
            x_copies[w][k - 1].wait_recv()
            piece = full.at[came, mine]
            for q in range(1, groups):
                copy = remote(
                    piece, piece, y_s, y_r, (w, k - 1, q - 1), {"groups": lax.rem(group + q, groups)}
                )
                copy.start()
                y_copies[w, k, q] = copy
                sends.append(copy)
            copy = remote(piece, piece, f_s, f_r, (w, k - 1, 0), {"dp": pair})
            copy.start()
            f_copies[w, k, 0] = copy
            sends.append(copy)
    for k in range(1, highs):
        came = lax.rem(high + highs - k, highs) * 2 + low
        for w, (own, full) in enumerate(weights):
            half = own.shape[1] // groups
            for q in range(1, groups):
                y_copies[w, k, q].wait_recv()
                theirs = lax.rem(group + groups - q, groups)
                piece = full.at[came, pl.ds(pl.multiple_of(theirs * half, half), half)]
                copy = remote(piece, piece, f_s, f_r, (w, k - 1, q), {"dp": pair})
                copy.start()
                f_copies[w, k, q] = copy
                sends.append(copy)
            add, src, acc = adders[w]
            add(came, False, src, acc)
    for k in range(1, highs):
        came = lax.rem(high + highs - k, highs) * 2 + other
        for w in range(2):
            for q in range(groups):
                f_copies[w, k, q].wait_recv()
            add, src, acc = adders[w]
            add(came, False, src, acc)

    act, d_hidden = silu_parts(acc_h[...], acc_d[...])
    act_h[...] = act
    dh_h[...] = d_hidden

    def home_block(block, carry):
        span = columns(block)
        out_h[:, span] = dot(act_h[...], down_w[block]).astype(BF16)
        din_h[:, span] = nt_dot(dh_h[...], up_w[block]).astype(BF16)
        return carry

    lax.fori_loop(0, slots, home_block, 0)

    for copy in d_copies:
        copy.wait_recv()

    acc_hv[...] = dot(vis_tok[:, 0:part], up_w[0])
    acc_dv[...] = nt_dot(vis_scl[:, 0:part], down_w[0])

    def visit_block(block, carry):
        add_up(block, False, vis_tok, acc_hv)
        add_down(block, False, vis_scl, acc_dv)
        return carry

    lax.fori_loop(1, slots, visit_block, 0)
    act, d_hidden = silu_parts(acc_hv[...], acc_dv[...])
    act_v[...] = act
    dh_v[...] = d_hidden

    r_copies = []

    def returns(array):
        for block in range(slots):
            span = pl.ds(block * part, part)
            if array == 0:
                src, dst = ret_out, back_out
                src[:, span] = dot(act_v[...], down_w[block]).astype(BF16)
            else:
                src, dst = ret_din, back_din
                src[:, span] = nt_dot(dh_v[...], up_w[block]).astype(BF16)
            for way, target in enumerate((before, after)):
                lines = pl.ds(way * CAP, CAP)
                copy = remote(
                    src.at[lines, span], dst.at[lines, span], r_s, r_r, (array, block, way),
                    {"expert": target},
                )
                copy.start()
                r_copies.append(copy)
                sends.append(copy)

    hidden_width = act_h.shape[1]

    def up_term(block, dst):
        step = min(256, part)

        def one(i, carry):
            span = pl.ds(pl.multiple_of(block * part + i * step, step), step)
            term = tn_dot(tok[:, span], dh_h[...]) + tn_dot(vis_tok[:, span], dh_v[...])
            dst[pl.ds(pl.multiple_of(i * step, step), step), :] = term.astype(dst.dtype)
            return carry

        lax.fori_loop(0, part // step, one, 0)

    def down_term(block, dst):
        step = 256
        span = columns(block)

        def one(i, carry):
            lines = pl.ds(pl.multiple_of(i * step, step), step)
            term = tn_dot(act_h[:, lines], home_scl[:, span]) + tn_dot(act_v[:, lines], vis_scl[:, span])
            dst[lines, :] = term.astype(dst.dtype)
            return carry

        lax.fori_loop(0, hidden_width // step, one, 0)

    terms = (
        (up_term, up_pair, up_pair_in, up_own, up_x, up_x_in, grad_up),
        (down_term, down_pair, down_pair_in, down_own, down_x, down_x_in, grad_down),
    )
    gp_copies = {}
    gx_copies = {}

    def make_terms(w, k):
        make, pair_out, pair_in, own = terms[w][:4]
        target = lax.rem(high + k, highs) * 2
        make(target + other, pair_out.at[k])
        copy = remote(pair_out.at[k], pair_in.at[k], gp_s, gp_r, (w, k), {"dp": pair})
        copy.start()
        gp_copies[w, k] = copy
        sends.append(copy)
        make(target + low, own.at[k])

    def send_x(w, k):
        pair_in, own, out, into = terms[w][2:6]
        gp_copies[w, k].wait_recv()
        out[k - 1] = (own[k] + pair_in[k].astype(F32)).astype(BF16)
        copy = remote(
            out.at[k - 1], into.at[k - 1], gx_s, gx_r, (w, k - 1),
            {"dp": lax.rem(high + k, highs) * 2 + low},
        )
        copy.start()
        gx_copies[w, k] = copy
        sends.append(copy)

    for k in range(1, highs):
        make_terms(0, k)
    returns(0)
    for k in range(1, highs):
        send_x(0, k)
    for k in range(1, highs):
        make_terms(1, k)
    returns(1)
    for k in range(1, highs):
        send_x(1, k)
    for w in range(2):
        make_terms(w, 0)
    for w in range(2):
        pair_in, own = terms[w][2:4]
        gp_copies[w, 0].wait_recv()
        own[0] = own[0] + pair_in[0].astype(F32)

    for copy in r_copies:
        copy.wait_recv()
    picked = pick[...]
    side = tn_dot(picked, back_out[...])
    mixed[...] = (home_gate * out_h[...].astype(F32) + side_gate * side).astype(BF16)
    side = tn_dot(picked, back_din[...])
    grad_tok[...] = (din_h[...].astype(F32) + side).astype(BF16)
    stores = []

    def store(src, dst):
        copy = pltpu.make_async_copy(src, dst, out_sem.at[len(stores)])
        copy.start()
        stores.append(copy)

    store(mixed, mixed_out)
    store(grad_tok, grad_tok_out)

    for w in range(2):
        own, _, into, result = terms[w][3:7]
        whole = own[0]
        for k in range(1, highs):
            gx_copies[w, k].wait_recv()
            whole = whole + into[k - 1].astype(F32)
        result[0] = whole.astype(BF16)
        store(result, (grad_up_out, grad_down_out)[w])
    for copy in stores:
        copy.wait()
    for copy in sends:
        copy.wait_send()


def hand_over(*refs):
    count = (len(refs) - 1) // 2
    sems = refs[-1]
    copies = []
    for i in range(count):
        src, dst = refs[i], refs[count + i]
        middle = src.shape[-2] // 2
        for j in range(2):
            span = pl.ds(j * middle, middle)
            if len(src.shape) == 3:
                pieces = (src.at[0, span], dst.at[0, span])
            else:
                pieces = (src.at[span], dst.at[span])
            copy = pltpu.make_async_copy(*pieces, sems.at[i, j])
            copy.start()
            copies.append(copy)
    for copy in copies:
        copy.wait()


def local(tokens, cotangent, expert_ids, gate_fix, w_up, w_down):
    rows, width = tokens.shape
    groups = lax.axis_size("groups")
    cycle = lax.axis_size("expert")
    slots = lax.axis_size("dp")
    highs = slots // 2
    hidden = w_up.shape[2]
    part = width // slots
    side = 2 * CAP
    vmem = pl.BlockSpec(memory_space=pltpu.VMEM)
    anywhere = pl.BlockSpec(memory_space=pl.ANY)
    dma = pltpu.SemaphoreType.DMA
    far = highs - 1
    results = (
        jax.ShapeDtypeStruct((rows, width), BF16),
        jax.ShapeDtypeStruct((rows, width), BF16),
        jax.ShapeDtypeStruct((1, part, hidden), BF16),
        jax.ShapeDtypeStruct((1, hidden, part), BF16),
    )
    made = pl.pallas_call(
        functools.partial(kernel, groups, cycle, slots),
        out_shape=results,
        in_specs=[vmem] * 4 + [anywhere] * 2,
        out_specs=[anywhere] * 4,
        scratch_shapes=[
            pltpu.VMEM((rows, width), BF16),
            pltpu.VMEM((rows, width), BF16),
            pltpu.VMEM((1, part, hidden), BF16),
            pltpu.VMEM((1, hidden, part), BF16),
            dma((4,)),
            pltpu.VMEM((slots, part, hidden), BF16),
            pltpu.VMEM((slots, hidden, part), BF16),
            pltpu.VMEM((side, rows), BF16),
            pltpu.VMEM((rows, width), BF16),
            pltpu.VMEM((side, width), BF16),
            pltpu.VMEM((side, width), BF16),
            pltpu.VMEM((side, width), BF16),
            pltpu.VMEM((side, width), BF16),
            pltpu.VMEM((rows, hidden), F32),
            pltpu.VMEM((rows, hidden), F32),
            pltpu.VMEM((side, hidden), F32),
            pltpu.VMEM((side, hidden), F32),
            pltpu.VMEM((rows, hidden), BF16),
            pltpu.VMEM((rows, hidden), BF16),
            pltpu.VMEM((side, hidden), BF16),
            pltpu.VMEM((side, hidden), BF16),
            pltpu.VMEM((rows, width), BF16),
            pltpu.VMEM((rows, width), BF16),
            pltpu.VMEM((side, width), BF16),
            pltpu.VMEM((side, width), BF16),
            pltpu.VMEM((side, width), BF16),
            pltpu.VMEM((side, width), BF16),
            pltpu.VMEM((highs, part, hidden), BF16),
            pltpu.VMEM((highs, hidden, part), BF16),
            pltpu.VMEM((highs, part, hidden), BF16),
            pltpu.VMEM((highs, hidden, part), BF16),
            pltpu.VMEM((highs, part, hidden), F32),
            pltpu.VMEM((highs, hidden, part), F32),
            pltpu.VMEM((far, part, hidden), BF16),
            pltpu.VMEM((far, hidden, part), BF16),
            pltpu.VMEM((far, part, hidden), BF16),
            pltpu.VMEM((far, hidden, part), BF16),
            dma((2,)),
            dma((2,)),
            dma((2,)),
            dma((2, far)),
            dma((2, far)),
            dma((2, far, groups - 1)),
            dma((2, far, groups - 1)),
            dma((2, far, groups)),
            dma((2, far, groups)),
            dma((2, 2)),
            dma((2, 2)),
            dma((2, slots, 2)),
            dma((2, slots, 2)),
            dma((2, highs)),
            dma((2, highs)),
            dma((2, far)),
            dma((2, far)),
        ],
        compiler_params=pltpu.CompilerParams(
            collective_id=0, has_side_effects=True, vmem_limit_bytes=56 * 1024 * 1024
        ),
    )(tokens, cotangent, expert_ids.T, gate_fix.T, w_up, w_down)
    return pl.pallas_call(
        hand_over,
        out_shape=results,
        in_specs=[anywhere] * 4,
        out_specs=[anywhere] * 4,
        scratch_shapes=[dma((4, 2))],
    )(*made)


def solution(mesh):
    in_specs = (
        P(("groups", "expert", "dp"), None),
        P(("groups", "expert", "dp"), None),
        P(("groups", "expert", "dp"), None),
        P(("groups", "expert", "dp"), None),
        P("expert", "dp", None),
        P("expert", None, "dp"),
    )
    out_specs = (
        P(("groups", "expert", "dp"), None),
        P(("groups", "expert", "dp"), None),
        P(("groups", "expert"), "dp", None),
        P(("groups", "expert"), None, "dp"),
    )
    return jax.shard_map(local, mesh=mesh, in_specs=in_specs, out_specs=out_specs, check_vma=False)
```

```python
import functools

import jax
import jax.numpy as jnp
from jax import lax
from jax.experimental import pallas as pl
from jax.experimental.pallas import tpu as pltpu
from jax.sharding import PartitionSpec as P

CAP = 80
MESH = pl.DeviceIdType.MESH
F32 = jnp.float32
BF16 = jnp.bfloat16


def nt_dot(left, right):
    return lax.dot_general(left, right, (((1,), (1,)), ((), ())), preferred_element_type=F32)


def tn_dot(left, right):
    return lax.dot_general(left, right, (((0,), (0,)), ((), ())), preferred_element_type=F32)


def dot(left, right):
    return jnp.dot(left, right, preferred_element_type=F32)


def remote(src, dst, sends, recvs, where, device):
    return pltpu.make_async_remote_copy(
        src_ref=src,
        dst_ref=dst,
        send_sem=sends.at[where],
        recv_sem=recvs.at[where],
        device_id=device,
        device_id_type=MESH,
    )


def kernel(
    groups, cycle, slots,
    tok, cot, ids, fix, up_in, down_in,
    mixed_out, grad_tok_out, grad_up_out, grad_down_out,
    mixed, grad_tok, grad_up, grad_down, out_sem,
    up_w, down_w, pick, home_scl, snd_tok, snd_scl, vis_tok, vis_scl,
    acc_h, acc_d, acc_hv, acc_dv, act_h, dh_h, act_v, dh_v, out_h, din_h,
    ret_out, ret_din, back_out, back_din,
    up_pair, down_pair, up_pair_in, down_pair_in, up_own, down_own,
    up_x, down_x, up_x_in, down_x_in,
    local_sem, pair_s, pair_r, x_s, x_r, y_s, y_r, f_s, f_r, d_s, d_r, r_s, r_r,
    gp_s, gp_r, gx_s, gx_r,
):
    rows = tok.shape[0]
    width = tok.shape[1]
    part = width // slots
    highs = slots // 2
    group = lax.axis_index("groups")
    place = lax.axis_index("expert")
    me = lax.axis_index("dp")
    high = me // 2
    low = me % 2
    other = 1 - low
    pair = high * 2 + other
    after = lax.rem(place + 1, cycle)
    before = lax.rem(place + cycle - 1, cycle)

    def columns(block):
        return pl.ds(pl.multiple_of(block * part, part), part)

    barrier = pltpu.get_barrier_semaphore()
    peers = [{"dp": pair}, {"expert": after}, {"expert": before}]
    peers += [{"dp": lax.rem(high + k, highs) * 2 + low} for k in range(1, highs)]
    peers += [{"groups": lax.rem(group + q, groups)} for q in range(1, groups)]
    for peer in peers:
        pl.semaphore_signal(barrier, inc=1, device_id=peer, device_id_type=MESH)

    lane = lax.broadcasted_iota(jnp.int32, (rows, rows), 1)
    line = lax.broadcasted_iota(jnp.int32, (rows, rows), 0)
    eye = jnp.where(line == lane, 1.0, 0.0).astype(BF16)
    goes = jnp.where(ids[1:2, :] == after, 1.0, 0.0).astype(F32)
    upper = lax.broadcasted_iota(jnp.int32, (8, rows), 0) == 0
    marks = jnp.where(upper, goes, 1.0 - goes)
    counts = dot(marks.astype(BF16), jnp.where(line <= lane, 1.0, 0.0).astype(BF16))
    slot = lax.broadcasted_iota(jnp.int32, (2 * CAP, rows), 0)
    first = slot < CAP
    wanted = jnp.where(first, slot, slot - CAP).astype(F32) + 1.0
    count = jnp.where(first, counts[0:1, :], counts[1:2, :])
    mark = jnp.where(first, marks[0:1, :], marks[1:2, :])
    pick[...] = jnp.where(count == wanted, mark, 0.0).astype(BF16)
    fixed = fix[...]
    split = jnp.concatenate([fixed // 256, fixed % 256], axis=0).astype(F32).astype(BF16)
    turned = nt_dot(eye, split)
    home_fix = turned[:, 0:1] * 256.0 + turned[:, 2:3]
    side_fix = turned[:, 1:2] * 256.0 + turned[:, 3:4]
    total = home_fix + side_fix
    home_gate = home_fix / total
    side_gate = side_fix / total

    sends = []

    def begin(copy):
        copy.start()
        sends.append(copy)
        return copy

    ways = ((0, after), (1, before))
    order = [(k, h) for k in list(range(1, highs)) + [0] for h in (other, low)]
    order = [lax.rem(high + k, highs) * 2 + h for k, h in order]
    far = 2 * (highs - 1)

    picked = pick[...]
    snd_tok[...] = dot(picked, tok[...]).astype(BF16)
    pl.semaphore_wait(barrier, len(peers))

    tok_copies = []
    for way, target in ways:
        span = pl.ds(way * CAP, CAP)
        copy = remote(snd_tok.at[span], vis_tok.at[span], d_s, d_r, (slots, way), {"expert": target})
        tok_copies.append(begin(copy))

    weights = ((up_in, up_w), (down_in, down_w))
    local_copies = []
    pair_copies = []
    x_copies = [[], []]
    for w, (own, full) in enumerate(weights):
        half = own.shape[1] // groups
        mine = pl.ds(pl.multiple_of(group * half, half), half)
        for k in range(1, highs):
            copy = remote(
                own.at[0, mine], full.at[me, mine], x_s, x_r, (w, k - 1),
                {"dp": lax.rem(high + k, highs) * 2 + low},
            )
            x_copies[w].append(begin(copy))
        copy = remote(own.at[0], full.at[me], pair_s, pair_r, w, {"dp": pair})
        pair_copies.append(begin(copy))
        copy = pltpu.make_async_copy(own.at[0], full.at[me], local_sem.at[w])
        copy.start()
        local_copies.append(copy)

    wide = cot[...].astype(F32)
    snd_scl[...] = dot(picked, (side_gate * wide).astype(BF16)).astype(BF16)
    scl_copies = []
    for r, block in enumerate(order):
        for way, target in ways:
            lines = pl.ds(way * CAP, CAP)
            copy = remote(
                snd_scl.at[lines, columns(block)], vis_scl.at[lines, columns(block)], d_s, d_r, (r, way),
                {"expert": target},
            )
            scl_copies.append(begin(copy))
    home_scl[...] = (home_gate * wide).astype(BF16)

    def add_up(block, first_one, src, acc):
        term = dot(src[:, columns(block)], up_w[block])
        acc[...] = term if first_one else acc[...] + term

    def add_down(block, first_one, src, acc):
        term = nt_dot(src[:, columns(block)], down_w[block])
        acc[...] = term if first_one else acc[...] + term

    def forward_x(w, k):
        own, full = weights[w]
        came = lax.rem(high + highs - k, highs) * 2 + low
        half = own.shape[1] // groups
        x_copies[w][k - 1].wait_recv()
        piece = full.at[came, pl.ds(pl.multiple_of(group * half, half), half)]
        for q in range(1, groups):
            y_copies[w, k, q] = begin(remote(
                piece, piece, y_s, y_r, (w, k - 1, q - 1), {"groups": lax.rem(group + q, groups)}
            ))
        f_copies[w, k, 0] = begin(remote(piece, piece, f_s, f_r, (w, k - 1, 0), {"dp": pair}))

    def forward_y(w, k):
        own, full = weights[w]
        came = lax.rem(high + highs - k, highs) * 2 + low
        half = own.shape[1] // groups
        for q in range(1, groups):
            y_copies[w, k, q].wait_recv()
            theirs = lax.rem(group + groups - q, groups)
            piece = full.at[came, pl.ds(pl.multiple_of(theirs * half, half), half)]
            f_copies[w, k, q] = begin(remote(piece, piece, f_s, f_r, (w, k - 1, q), {"dp": pair}))

    y_copies = {}
    f_copies = {}
    local_copies[0].wait()
    add_up(me, True, tok, acc_h)
    pair_copies[0].wait_recv()
    add_up(pair, False, tok, acc_h)
    local_copies[1].wait()
    add_down(me, True, home_scl, acc_d)
    for k in range(1, highs):
        forward_x(0, k)
    pair_copies[1].wait_recv()
    add_down(pair, False, home_scl, acc_d)
    for copy in tok_copies:
        copy.wait_recv()
    add_up(me, True, vis_tok, acc_hv)
    add_up(pair, False, vis_tok, acc_hv)
    for k in range(1, highs):
        forward_x(1, k)
    for k in range(1, highs):
        forward_y(0, k)
        came = lax.rem(high + highs - k, highs) * 2 + low
        add_up(came, False, tok, acc_h)
        add_up(came, False, vis_tok, acc_hv)
    for k in range(1, highs):
        for q in range(groups):
            f_copies[0, k, q].wait_recv()
        came = lax.rem(high + highs - k, highs) * 2 + other
        add_up(came, False, tok, acc_h)
        add_up(came, False, vis_tok, acc_hv)

    def activate(acc, act):
        hidden = acc[...]
        act[...] = (hidden * (1.0 / (1.0 + jnp.exp(-hidden)))).astype(BF16)

    def back_through(acc, d_acc, out):
        hidden = acc[...]
        sig = 1.0 / (1.0 + jnp.exp(-hidden))
        out[...] = (d_acc[...] * sig * (1.0 + hidden * (1.0 - sig))).astype(BF16)

    activate(acc_h, act_h)
    activate(acc_hv, act_v)

    def home_block(block, carry):
        span = columns(block)
        out_h[:, span] = dot(act_h[...], down_w[block]).astype(BF16)
        din_h[:, span] = nt_dot(dh_h[...], up_w[block]).astype(BF16)
        return carry

    r_copies = [[], []]

    def returns(array):
        for block in range(slots):
            span = pl.ds(block * part, part)
            if array == 0:
                src, dst = ret_out, back_out
                src[:, span] = dot(act_v[...], down_w[block]).astype(BF16)
            else:
                src, dst = ret_din, back_din
                src[:, span] = nt_dot(dh_v[...], up_w[block]).astype(BF16)
            for way, target in enumerate((before, after)):
                lines = pl.ds(way * CAP, CAP)
                r_copies[array].append(begin(remote(
                    src.at[lines, span], dst.at[lines, span], r_s, r_r, (array, block, way),
                    {"expert": target},
                )))

    hidden_width = act_h.shape[1]

    def up_term(block, dst):
        step = min(256, part)

        def one(i, carry):
            span = pl.ds(pl.multiple_of(block * part + i * step, step), step)
            term = tn_dot(tok[:, span], dh_h[...]) + tn_dot(vis_tok[:, span], dh_v[...])
            dst[pl.ds(pl.multiple_of(i * step, step), step), :] = term.astype(dst.dtype)
            return carry

        lax.fori_loop(0, part // step, one, 0)

    def down_term(block, dst):
        step = 256
        span = columns(block)

        def one(i, carry):
            lines = pl.ds(pl.multiple_of(i * step, step), step)
            term = tn_dot(act_h[:, lines], home_scl[:, span]) + tn_dot(act_v[:, lines], vis_scl[:, span])
            dst[lines, :] = term.astype(dst.dtype)
            return carry

        lax.fori_loop(0, hidden_width // step, one, 0)

    terms = (
        (up_term, up_pair, up_pair_in, up_own, up_x, up_x_in, grad_up),
        (down_term, down_pair, down_pair_in, down_own, down_x, down_x_in, grad_down),
    )
    gp_copies = {}
    gx_copies = {}

    def make_terms(w, k):
        make, pair_out, pair_in, own = terms[w][:4]
        target = lax.rem(high + k, highs) * 2
        make(target + other, pair_out.at[k])
        copy = remote(pair_out.at[k], pair_in.at[k], gp_s, gp_r, (w, k), {"dp": pair})
        copy.start()
        gp_copies[w, k] = copy
        sends.append(copy)
        make(target + low, own.at[k])

    def send_x(w, k):
        pair_in, own, out, into = terms[w][2:6]
        gp_copies[w, k].wait_recv()
        out[k - 1] = (own[k] + pair_in[k].astype(F32)).astype(BF16)
        copy = remote(
            out.at[k - 1], into.at[k - 1], gx_s, gx_r, (w, k - 1),
            {"dp": lax.rem(high + k, highs) * 2 + low},
        )
        copy.start()
        gx_copies[w, k] = copy
        sends.append(copy)

    for copy in scl_copies[: 2 * far]:
        copy.wait_recv()
    for k in range(1, highs):
        make_terms(1, k)
    for k in range(1, highs):
        forward_y(1, k)
    for k in range(1, highs):
        send_x(1, k)
    for k in range(1, highs):
        add_down(lax.rem(high + highs - k, highs) * 2 + low, False, home_scl, acc_d)
    for k in range(1, highs):
        for q in range(groups):
            f_copies[1, k, q].wait_recv()
        add_down(lax.rem(high + highs - k, highs) * 2 + other, False, home_scl, acc_d)
    returns(0)
    back_through(acc_h, acc_d, dh_h)
    for r, block in enumerate(order[:far]):
        add_down(block, r == 0, vis_scl, acc_dv)
    for copy in scl_copies[2 * far :]:
        copy.wait_recv()
    for block in order[far:]:
        add_down(block, False, vis_scl, acc_dv)
    back_through(acc_hv, acc_dv, dh_v)
    for k in range(1, highs):
        make_terms(0, k)
    returns(1)
    for k in range(1, highs):
        send_x(0, k)
    for w in (1, 0):
        make_terms(w, 0)
    lax.fori_loop(0, slots, home_block, 0)
    for w in (1, 0):
        pair_in, own = terms[w][2:4]
        gp_copies[w, 0].wait_recv()
        own[0] = own[0] + pair_in[0].astype(F32)

    stores = []

    def store(src, dst):
        copy = pltpu.make_async_copy(src, dst, out_sem.at[len(stores)])
        copy.start()
        stores.append(copy)

    def finish(w):
        own, _, into, result = terms[w][3:7]
        whole = own[0]
        for k in range(1, highs):
            gx_copies[w, k].wait_recv()
            whole = whole + into[k - 1].astype(F32)
        result[0] = whole.astype(BF16)
        store(result, (grad_up_out, grad_down_out)[w])

    picked = pick[...]
    for copy in r_copies[0]:
        copy.wait_recv()
    side = tn_dot(picked, back_out[...])
    mixed[...] = (home_gate * out_h[...].astype(F32) + side_gate * side).astype(BF16)
    store(mixed, mixed_out)
    finish(1)
    for copy in r_copies[1]:
        copy.wait_recv()
    side = tn_dot(picked, back_din[...])
    grad_tok[...] = (din_h[...].astype(F32) + side).astype(BF16)
    store(grad_tok, grad_tok_out)
    finish(0)
    for copy in stores:
        copy.wait()
    for copy in sends:
        copy.wait_send()


def hand_over(*refs):
    count = (len(refs) - 2) // 3
    sems, done = refs[-2:]
    loads, stores = [], []

    def piece(ref, j):
        middle = ref.shape[-2] // 2
        span = pl.ds(j * middle, middle)
        return ref.at[0, span] if len(ref.shape) == 3 else ref.at[span]

    for i in range(count):
        for j in range(2):
            copy = pltpu.make_async_copy(piece(refs[i], j), piece(refs[2 * count + i], j), sems.at[i, j])
            copy.start()
            loads.append(copy)
    for i in range(count):
        for j in range(2):
            loads[2 * i + j].wait()
            copy = pltpu.make_async_copy(
                piece(refs[2 * count + i], j), piece(refs[count + i], j), done.at[i, j]
            )
            copy.start()
            stores.append(copy)
    for copy in stores:
        copy.wait()


def local(tokens, cotangent, expert_ids, gate_fix, w_up, w_down):
    rows, width = tokens.shape
    groups = lax.axis_size("groups")
    cycle = lax.axis_size("expert")
    slots = lax.axis_size("dp")
    highs = slots // 2
    hidden = w_up.shape[2]
    part = width // slots
    side = 2 * CAP
    vmem = pl.BlockSpec(memory_space=pltpu.VMEM)
    anywhere = pl.BlockSpec(memory_space=pl.ANY)
    dma = pltpu.SemaphoreType.DMA
    far = highs - 1
    results = (
        jax.ShapeDtypeStruct((rows, width), BF16),
        jax.ShapeDtypeStruct((rows, width), BF16),
        jax.ShapeDtypeStruct((1, part, hidden), BF16),
        jax.ShapeDtypeStruct((1, hidden, part), BF16),
    )
    made = pl.pallas_call(
        functools.partial(kernel, groups, cycle, slots),
        out_shape=results,
        in_specs=[vmem] * 4 + [anywhere] * 2,
        out_specs=[anywhere] * 4,
        scratch_shapes=[
            pltpu.VMEM((rows, width), BF16),
            pltpu.VMEM((rows, width), BF16),
            pltpu.VMEM((1, part, hidden), BF16),
            pltpu.VMEM((1, hidden, part), BF16),
            dma((4,)),
            pltpu.VMEM((slots, part, hidden), BF16),
            pltpu.VMEM((slots, hidden, part), BF16),
            pltpu.VMEM((side, rows), BF16),
            pltpu.VMEM((rows, width), BF16),
            pltpu.VMEM((side, width), BF16),
            pltpu.VMEM((side, width), BF16),
            pltpu.VMEM((side, width), BF16),
            pltpu.VMEM((side, width), BF16),
            pltpu.VMEM((rows, hidden), F32),
            pltpu.VMEM((rows, hidden), F32),
            pltpu.VMEM((side, hidden), F32),
            pltpu.VMEM((side, hidden), F32),
            pltpu.VMEM((rows, hidden), BF16),
            pltpu.VMEM((rows, hidden), BF16),
            pltpu.VMEM((side, hidden), BF16),
            pltpu.VMEM((side, hidden), BF16),
            pltpu.VMEM((rows, width), BF16),
            pltpu.VMEM((rows, width), BF16),
            pltpu.VMEM((side, width), BF16),
            pltpu.VMEM((side, width), BF16),
            pltpu.VMEM((side, width), BF16),
            pltpu.VMEM((side, width), BF16),
            pltpu.VMEM((highs, part, hidden), BF16),
            pltpu.VMEM((highs, hidden, part), BF16),
            pltpu.VMEM((highs, part, hidden), BF16),
            pltpu.VMEM((highs, hidden, part), BF16),
            pltpu.VMEM((highs, part, hidden), F32),
            pltpu.VMEM((highs, hidden, part), F32),
            pltpu.VMEM((far, part, hidden), BF16),
            pltpu.VMEM((far, hidden, part), BF16),
            pltpu.VMEM((far, part, hidden), BF16),
            pltpu.VMEM((far, hidden, part), BF16),
            dma((2,)),
            dma((2,)),
            dma((2,)),
            dma((2, far)),
            dma((2, far)),
            dma((2, far, groups - 1)),
            dma((2, far, groups - 1)),
            dma((2, far, groups)),
            dma((2, far, groups)),
            dma((slots + 1, 2)),
            dma((slots + 1, 2)),
            dma((2, slots, 2)),
            dma((2, slots, 2)),
            dma((2, highs)),
            dma((2, highs)),
            dma((2, far)),
            dma((2, far)),
        ],
        compiler_params=pltpu.CompilerParams(
            collective_id=0, has_side_effects=True, vmem_limit_bytes=56 * 1024 * 1024
        ),
    )(tokens, cotangent, expert_ids.T, gate_fix.T, w_up, w_down)
    return pl.pallas_call(
        hand_over,
        out_shape=results,
        in_specs=[anywhere] * 4,
        out_specs=[anywhere] * 4,
        scratch_shapes=[pltpu.VMEM(shape.shape, BF16) for shape in results] + [dma((4, 2)), dma((4, 2))],
    )(*made)


def solution(mesh):
    in_specs = (
        P(("groups", "expert", "dp"), None),
        P(("groups", "expert", "dp"), None),
        P(("groups", "expert", "dp"), None),
        P(("groups", "expert", "dp"), None),
        P("expert", "dp", None),
        P("expert", None, "dp"),
    )
    out_specs = (
        P(("groups", "expert", "dp"), None),
        P(("groups", "expert", "dp"), None),
        P(("groups", "expert"), "dp", None),
        P(("groups", "expert"), None, "dp"),
    )
    return jax.shard_map(local, mesh=mesh, in_specs=in_specs, out_specs=out_specs, check_vma=False)
```

```python
import functools

import jax
import jax.numpy as jnp
from jax import lax
from jax.experimental import pallas as pl
from jax.experimental.pallas import tpu as pltpu
from jax.sharding import PartitionSpec as P

CAP = 80
HALVES = 2
MESH = pl.DeviceIdType.MESH
F32 = jnp.float32
BF16 = jnp.bfloat16


def nt_dot(left, right):
    return lax.dot_general(left, right, (((1,), (1,)), ((), ())), preferred_element_type=F32)


def tn_dot(left, right):
    return lax.dot_general(left, right, (((0,), (0,)), ((), ())), preferred_element_type=F32)


def dot(left, right):
    return jnp.dot(left, right, preferred_element_type=F32)


def remote(src, dst, sends, recvs, where, device):
    return pltpu.make_async_remote_copy(
        src_ref=src,
        dst_ref=dst,
        send_sem=sends.at[where],
        recv_sem=recvs.at[where],
        device_id=device,
        device_id_type=MESH,
    )


def kernel(
    groups, cycle, slots,
    tok, cot, ids, fix, up_in, down_in,
    mixed_out, grad_tok_out, grad_up_out, grad_down_out,
    mixed, grad_tok, grad_up, grad_down, out_sem,
    up_w, down_w, pick, home_scl, snd_tok, snd_scl, vis_tok, vis_scl,
    acc_h, acc_d, acc_hv, acc_dv, act_h, dh_h, act_v, dh_v, out_h, din_h,
    ret_out, ret_din, back_out, back_din,
    up_pair, down_pair, up_pair_in, down_pair_in, up_own, down_own,
    up_x, down_x, up_x_in, down_x_in,
    local_sem, pair_s, pair_r, x_s, x_r, y_s, y_r, f_s, f_r, d_s, d_r, r_s, r_r,
    gp_s, gp_r, gx_s, gx_r,
):
    rows = tok.shape[0]
    width = tok.shape[1]
    part = width // slots
    highs = slots // 2
    group = lax.axis_index("groups")
    place = lax.axis_index("expert")
    me = lax.axis_index("dp")
    high = me // 2
    low = me % 2
    other = 1 - low
    pair = high * 2 + other
    after = lax.rem(place + 1, cycle)
    before = lax.rem(place + cycle - 1, cycle)

    def columns(block):
        return pl.ds(pl.multiple_of(block * part, part), part)

    barrier = pltpu.get_barrier_semaphore()
    peers = [{"dp": pair}, {"expert": after}, {"expert": before}]
    peers += [{"dp": lax.rem(high + k, highs) * 2 + low} for k in range(1, highs)]
    peers += [{"groups": lax.rem(group + q, groups)} for q in range(1, groups)]
    for peer in peers:
        pl.semaphore_signal(barrier, inc=1, device_id=peer, device_id_type=MESH)

    lane = lax.broadcasted_iota(jnp.int32, (rows, rows), 1)
    line = lax.broadcasted_iota(jnp.int32, (rows, rows), 0)
    eye = jnp.where(line == lane, 1.0, 0.0).astype(BF16)
    goes = jnp.where(ids[1:2, :] == after, 1.0, 0.0).astype(F32)
    upper = lax.broadcasted_iota(jnp.int32, (8, rows), 0) == 0
    marks = jnp.where(upper, goes, 1.0 - goes)
    counts = dot(marks.astype(BF16), jnp.where(line <= lane, 1.0, 0.0).astype(BF16))
    slot = lax.broadcasted_iota(jnp.int32, (2 * CAP, rows), 0)
    first = slot < CAP
    wanted = jnp.where(first, slot, slot - CAP).astype(F32) + 1.0
    count = jnp.where(first, counts[0:1, :], counts[1:2, :])
    mark = jnp.where(first, marks[0:1, :], marks[1:2, :])
    pick[...] = jnp.where(count == wanted, mark, 0.0).astype(BF16)
    fixed = fix[...]
    split = jnp.concatenate([fixed // 256, fixed % 256], axis=0).astype(F32).astype(BF16)
    turned = nt_dot(eye, split)
    home_fix = turned[:, 0:1] * 256.0 + turned[:, 2:3]
    side_fix = turned[:, 1:2] * 256.0 + turned[:, 3:4]
    total = home_fix + side_fix
    home_gate = home_fix / total
    side_gate = side_fix / total

    sends = []

    def begin(copy):
        copy.start()
        sends.append(copy)
        return copy

    ways = ((0, after), (1, before))
    order = [(k, h) for k in list(range(1, highs)) + [0] for h in (other, low)]
    order = [lax.rem(high + k, highs) * 2 + h for k, h in order]
    far = 2 * (highs - 1)
    part_half = part // HALVES
    pieces = [(block, m) for m in range(HALVES) for block in order[:far]]
    pieces += [(block, m) for m in range(HALVES) for block in order[far:]]

    picked = pick[...]
    snd_tok[...] = dot(picked, tok[...]).astype(BF16)
    pl.semaphore_wait(barrier, len(peers))

    tok_copies = []
    for way, target in ways:
        span = pl.ds(way * CAP, CAP)
        copy = remote(snd_tok.at[span], vis_tok.at[span], d_s, d_r, (slots * HALVES, way), {"expert": target})
        tok_copies.append(begin(copy))

    weights = ((up_in, up_w), (down_in, down_w))
    local_copies = []
    pair_copies = []
    x_copies = [[], []]
    for w, (own, full) in enumerate(weights):
        half = own.shape[1] // groups
        mine = pl.ds(pl.multiple_of(group * half, half), half)
        for k in range(1, highs):
            copy = remote(
                own.at[0, mine], full.at[me, mine], x_s, x_r, (w, k - 1),
                {"dp": lax.rem(high + k, highs) * 2 + low},
            )
            x_copies[w].append(begin(copy))
        copy = remote(own.at[0], full.at[me], pair_s, pair_r, w, {"dp": pair})
        pair_copies.append(begin(copy))
        copy = pltpu.make_async_copy(own.at[0], full.at[me], local_sem.at[w])
        copy.start()
        local_copies.append(copy)

    wide = cot[...].astype(F32)
    snd_scl[...] = dot(picked, (side_gate * wide).astype(BF16)).astype(BF16)
    scl_copies = []
    for r, (block, m) in enumerate(pieces):
        span = pl.ds(pl.multiple_of(block * part + m * part_half, part_half), part_half)
        for way, target in ways:
            lines = pl.ds(way * CAP, CAP)
            copy = remote(
                snd_scl.at[lines, span], vis_scl.at[lines, span], d_s, d_r, (r, way), {"expert": target}
            )
            scl_copies.append(begin(copy))
    home_scl[...] = (home_gate * wide).astype(BF16)

    def add_up(block, first_one, src, acc):
        term = dot(src[:, columns(block)], up_w[block])
        acc[...] = term if first_one else acc[...] + term

    def add_down(block, first_one, src, acc):
        term = nt_dot(src[:, columns(block)], down_w[block])
        acc[...] = term if first_one else acc[...] + term

    def forward_x(w, k):
        own, full = weights[w]
        came = lax.rem(high + highs - k, highs) * 2 + low
        half = own.shape[1] // groups
        x_copies[w][k - 1].wait_recv()
        piece = full.at[came, pl.ds(pl.multiple_of(group * half, half), half)]
        for q in range(1, groups):
            y_copies[w, k, q] = begin(remote(
                piece, piece, y_s, y_r, (w, k - 1, q - 1), {"groups": lax.rem(group + q, groups)}
            ))
        f_copies[w, k, 0] = begin(remote(piece, piece, f_s, f_r, (w, k - 1, 0), {"dp": pair}))

    def forward_y(w, k):
        own, full = weights[w]
        came = lax.rem(high + highs - k, highs) * 2 + low
        half = own.shape[1] // groups
        for q in range(1, groups):
            y_copies[w, k, q].wait_recv()
            theirs = lax.rem(group + groups - q, groups)
            piece = full.at[came, pl.ds(pl.multiple_of(theirs * half, half), half)]
            f_copies[w, k, q] = begin(remote(piece, piece, f_s, f_r, (w, k - 1, q), {"dp": pair}))

    y_copies = {}
    f_copies = {}
    local_copies[0].wait()
    add_up(me, True, tok, acc_h)
    pair_copies[0].wait_recv()
    add_up(pair, False, tok, acc_h)
    local_copies[1].wait()
    add_down(me, True, home_scl, acc_d)
    for k in range(1, highs):
        forward_x(0, k)
    pair_copies[1].wait_recv()
    add_down(pair, False, home_scl, acc_d)
    for copy in tok_copies:
        copy.wait_recv()
    add_up(me, True, vis_tok, acc_hv)
    add_up(pair, False, vis_tok, acc_hv)
    for k in range(1, highs):
        forward_x(1, k)
    for k in range(1, highs):
        forward_y(0, k)
        came = lax.rem(high + highs - k, highs) * 2 + low
        add_up(came, False, tok, acc_h)
        add_up(came, False, vis_tok, acc_hv)
    for k in range(1, highs):
        for q in range(groups):
            f_copies[0, k, q].wait_recv()
        came = lax.rem(high + highs - k, highs) * 2 + other
        add_up(came, False, tok, acc_h)
        add_up(came, False, vis_tok, acc_hv)

    def activate(acc, act):
        hidden = acc[...]
        act[...] = (hidden * (1.0 / (1.0 + jnp.exp(-hidden)))).astype(BF16)

    def back_through(acc, d_acc, out):
        hidden = acc[...]
        sig = 1.0 / (1.0 + jnp.exp(-hidden))
        out[...] = (d_acc[...] * sig * (1.0 + hidden * (1.0 - sig))).astype(BF16)

    activate(acc_h, act_h)
    activate(acc_hv, act_v)

    def home_block(block, carry):
        span = columns(block)
        out_h[:, span] = dot(act_h[...], down_w[block]).astype(BF16)
        din_h[:, span] = nt_dot(dh_h[...], up_w[block]).astype(BF16)
        return carry

    r_copies = [[], []]

    def returns(array):
        for block in range(slots):
            span = pl.ds(block * part, part)
            if array == 0:
                src, dst = ret_out, back_out
                src[:, span] = dot(act_v[...], down_w[block]).astype(BF16)
            else:
                src, dst = ret_din, back_din
                src[:, span] = nt_dot(dh_v[...], up_w[block]).astype(BF16)
            for way, target in enumerate((before, after)):
                lines = pl.ds(way * CAP, CAP)
                r_copies[array].append(begin(remote(
                    src.at[lines, span], dst.at[lines, span], r_s, r_r, (array, block, way),
                    {"expert": target},
                )))

    hidden_width = act_h.shape[1]

    def up_term(block, m, dst):
        step = min(256, part_half)

        def one(i, carry):
            start = m * part_half + i * step
            span = pl.ds(pl.multiple_of(block * part + start, step), step)
            term = tn_dot(tok[:, span], dh_h[...]) + tn_dot(vis_tok[:, span], dh_v[...])
            dst[pl.ds(pl.multiple_of(start, step), step), :] = term.astype(dst.dtype)
            return carry

        lax.fori_loop(0, part_half // step, one, 0)

    def down_term(block, m, dst):
        step = 256
        span = pl.ds(pl.multiple_of(block * part + m * part_half, part_half), part_half)
        into = pl.ds(m * part_half, part_half)

        def one(i, carry):
            lines = pl.ds(pl.multiple_of(i * step, step), step)
            term = tn_dot(act_h[:, lines], home_scl[:, span]) + tn_dot(act_v[:, lines], vis_scl[:, span])
            dst[lines, into] = term.astype(dst.dtype)
            return carry

        lax.fori_loop(0, hidden_width // step, one, 0)

    def cut(w, k, m):
        span = pl.ds(m * part_half, part_half)
        return (k, span) if w == 0 else (k, slice(None), span)

    terms = (
        (up_term, up_pair, up_pair_in, up_own, up_x, up_x_in, grad_up),
        (down_term, down_pair, down_pair_in, down_own, down_x, down_x_in, grad_down),
    )
    gp_copies = {}
    gx_copies = {}

    def make_terms(w, k, m):
        make, pair_out, pair_in, own = terms[w][:4]
        target = lax.rem(high + k, highs) * 2
        make(target + other, m, pair_out.at[k])
        where = cut(w, k, m)
        gp_copies[w, k, m] = begin(remote(
            pair_out.at[where], pair_in.at[where], gp_s, gp_r, (w, k, m), {"dp": pair}
        ))
        make(target + low, m, own.at[k])

    def send_x(w, k, m):
        pair_in, own, out, into = terms[w][2:6]
        gp_copies[w, k, m].wait_recv()
        where = cut(w, k, m)
        there = cut(w, k - 1, m)
        out[there] = (own[where] + pair_in[where].astype(F32)).astype(BF16)
        gx_copies[w, k, m] = begin(remote(
            out.at[there], into.at[there], gx_s, gx_r, (w, k - 1, m),
            {"dp": lax.rem(high + k, highs) * 2 + low},
        ))

    for m in range(HALVES):
        for copy in scl_copies[2 * far * m : 2 * far * (m + 1)]:
            copy.wait_recv()
        for k in range(1, highs):
            make_terms(1, k, m)
        for k in range(1, highs):
            send_x(1, k, m)
    for k in range(1, highs):
        forward_y(1, k)
    for k in range(1, highs):
        add_down(lax.rem(high + highs - k, highs) * 2 + low, False, home_scl, acc_d)
    for k in range(1, highs):
        for q in range(groups):
            f_copies[1, k, q].wait_recv()
        add_down(lax.rem(high + highs - k, highs) * 2 + other, False, home_scl, acc_d)
    returns(0)
    back_through(acc_h, acc_d, dh_h)
    for r, block in enumerate(order[:far]):
        add_down(block, r == 0, vis_scl, acc_dv)
    for copy in scl_copies[2 * far * HALVES :]:
        copy.wait_recv()
    for block in order[far:]:
        add_down(block, False, vis_scl, acc_dv)
    back_through(acc_hv, acc_dv, dh_v)
    for m in range(HALVES):
        for k in range(1, highs):
            make_terms(0, k, m)
        for k in range(1, highs):
            send_x(0, k, m)
    returns(1)
    for w in (1, 0):
        for m in range(HALVES):
            make_terms(w, 0, m)
    lax.fori_loop(0, slots, home_block, 0)
    for w in (1, 0):
        pair_in, own = terms[w][2:4]
        for m in range(HALVES):
            gp_copies[w, 0, m].wait_recv()
        own[0] = own[0] + pair_in[0].astype(F32)

    stores = []

    def store(src, dst):
        copy = pltpu.make_async_copy(src, dst, out_sem.at[len(stores)])
        copy.start()
        stores.append(copy)

    def finish(w, m):
        own, _, into, result = terms[w][3:7]
        where = cut(w, 0, m)
        whole = own[where]
        for k in range(1, highs):
            gx_copies[w, k, m].wait_recv()
            whole = whole + into[cut(w, k - 1, m)].astype(F32)
        result[where] = whole.astype(BF16)
        store(result.at[where], (grad_up_out, grad_down_out)[w].at[where])

    picked = pick[...]

    def combine(array, block):
        for copy in r_copies[array][2 * block : 2 * block + 2]:
            copy.wait_recv()
        span = pl.ds(block * part, part)
        if array == 0:
            side = tn_dot(picked, back_out[:, span])
            value = home_gate * out_h[:, span].astype(F32) + side_gate * side
            mixed[:, span] = value.astype(BF16)
        else:
            side = tn_dot(picked, back_din[:, span])
            grad_tok[:, span] = (din_h[:, span].astype(F32) + side).astype(BF16)

    for block in range(slots):
        combine(0, block)
    store(mixed, mixed_out)
    for m in range(HALVES):
        finish(1, m)
    for m in range(HALVES - 1):
        finish(0, m)
    for block in range(slots):
        combine(1, block)
    store(grad_tok, grad_tok_out)
    finish(0, HALVES - 1)
    for copy in stores:
        copy.wait()
    for copy in sends:
        copy.wait_send()


def hand_over(*refs):
    count = (len(refs) - 2) // 3
    sems, done = refs[-2:]
    loads, stores = [], []

    def piece(ref, j):
        middle = ref.shape[-2] // 2
        span = pl.ds(j * middle, middle)
        return ref.at[0, span] if len(ref.shape) == 3 else ref.at[span]

    for i in range(count):
        for j in range(2):
            copy = pltpu.make_async_copy(piece(refs[i], j), piece(refs[2 * count + i], j), sems.at[i, j])
            copy.start()
            loads.append(copy)
    for i in range(count):
        for j in range(2):
            loads[2 * i + j].wait()
            copy = pltpu.make_async_copy(
                piece(refs[2 * count + i], j), piece(refs[count + i], j), done.at[i, j]
            )
            copy.start()
            stores.append(copy)
    for copy in stores:
        copy.wait()


def local(tokens, cotangent, expert_ids, gate_fix, w_up, w_down):
    rows, width = tokens.shape
    groups = lax.axis_size("groups")
    cycle = lax.axis_size("expert")
    slots = lax.axis_size("dp")
    highs = slots // 2
    hidden = w_up.shape[2]
    part = width // slots
    side = 2 * CAP
    vmem = pl.BlockSpec(memory_space=pltpu.VMEM)
    anywhere = pl.BlockSpec(memory_space=pl.ANY)
    dma = pltpu.SemaphoreType.DMA
    far = highs - 1
    results = (
        jax.ShapeDtypeStruct((rows, width), BF16),
        jax.ShapeDtypeStruct((rows, width), BF16),
        jax.ShapeDtypeStruct((1, part, hidden), BF16),
        jax.ShapeDtypeStruct((1, hidden, part), BF16),
    )
    made = pl.pallas_call(
        functools.partial(kernel, groups, cycle, slots),
        out_shape=results,
        in_specs=[vmem] * 4 + [anywhere] * 2,
        out_specs=[anywhere] * 4,
        scratch_shapes=[
            pltpu.VMEM((rows, width), BF16),
            pltpu.VMEM((rows, width), BF16),
            pltpu.VMEM((1, part, hidden), BF16),
            pltpu.VMEM((1, hidden, part), BF16),
            dma((2 + 2 * HALVES,)),
            pltpu.VMEM((slots, part, hidden), BF16),
            pltpu.VMEM((slots, hidden, part), BF16),
            pltpu.VMEM((side, rows), BF16),
            pltpu.VMEM((rows, width), BF16),
            pltpu.VMEM((side, width), BF16),
            pltpu.VMEM((side, width), BF16),
            pltpu.VMEM((side, width), BF16),
            pltpu.VMEM((side, width), BF16),
            pltpu.VMEM((rows, hidden), F32),
            pltpu.VMEM((rows, hidden), F32),
            pltpu.VMEM((side, hidden), F32),
            pltpu.VMEM((side, hidden), F32),
            pltpu.VMEM((rows, hidden), BF16),
            pltpu.VMEM((rows, hidden), BF16),
            pltpu.VMEM((side, hidden), BF16),
            pltpu.VMEM((side, hidden), BF16),
            pltpu.VMEM((rows, width), BF16),
            pltpu.VMEM((rows, width), BF16),
            pltpu.VMEM((side, width), BF16),
            pltpu.VMEM((side, width), BF16),
            pltpu.VMEM((side, width), BF16),
            pltpu.VMEM((side, width), BF16),
            pltpu.VMEM((highs, part, hidden), BF16),
            pltpu.VMEM((highs, hidden, part), BF16),
            pltpu.VMEM((highs, part, hidden), BF16),
            pltpu.VMEM((highs, hidden, part), BF16),
            pltpu.VMEM((highs, part, hidden), F32),
            pltpu.VMEM((highs, hidden, part), F32),
            pltpu.VMEM((far, part, hidden), BF16),
            pltpu.VMEM((far, hidden, part), BF16),
            pltpu.VMEM((far, part, hidden), BF16),
            pltpu.VMEM((far, hidden, part), BF16),
            dma((2,)),
            dma((2,)),
            dma((2,)),
            dma((2, far)),
            dma((2, far)),
            dma((2, far, groups - 1)),
            dma((2, far, groups - 1)),
            dma((2, far, groups)),
            dma((2, far, groups)),
            dma((slots * HALVES + 1, 2)),
            dma((slots * HALVES + 1, 2)),
            dma((2, slots, 2)),
            dma((2, slots, 2)),
            dma((2, highs, HALVES)),
            dma((2, highs, HALVES)),
            dma((2, far, HALVES)),
            dma((2, far, HALVES)),
        ],
        compiler_params=pltpu.CompilerParams(
            collective_id=0, has_side_effects=True, vmem_limit_bytes=56 * 1024 * 1024
        ),
    )(tokens, cotangent, expert_ids.T, gate_fix.T, w_up, w_down)
    return pl.pallas_call(
        hand_over,
        out_shape=results,
        in_specs=[anywhere] * 4,
        out_specs=[anywhere] * 4,
        scratch_shapes=[pltpu.VMEM(shape.shape, BF16) for shape in results] + [dma((4, 2)), dma((4, 2))],
    )(*made)


def solution(mesh):
    in_specs = (
        P(("groups", "expert", "dp"), None),
        P(("groups", "expert", "dp"), None),
        P(("groups", "expert", "dp"), None),
        P(("groups", "expert", "dp"), None),
        P("expert", "dp", None),
        P("expert", None, "dp"),
    )
    out_specs = (
        P(("groups", "expert", "dp"), None),
        P(("groups", "expert", "dp"), None),
        P(("groups", "expert"), "dp", None),
        P(("groups", "expert"), None, "dp"),
    )
    return jax.shard_map(local, mesh=mesh, in_specs=in_specs, out_specs=out_specs, check_vma=False)
```

```python
import functools

import jax
import jax.numpy as jnp
from jax import lax
from jax.experimental import pallas as pl
from jax.experimental.pallas import tpu as pltpu
from jax.sharding import PartitionSpec as P

CAP = 80
HALVES = 2
MESH = pl.DeviceIdType.MESH
F32 = jnp.float32
BF16 = jnp.bfloat16


def nt_dot(left, right):
    return lax.dot_general(left, right, (((1,), (1,)), ((), ())), preferred_element_type=F32)


def tn_dot(left, right):
    return lax.dot_general(left, right, (((0,), (0,)), ((), ())), preferred_element_type=F32)


def dot(left, right):
    return jnp.dot(left, right, preferred_element_type=F32)


def remote(src, dst, sends, recvs, where, device):
    return pltpu.make_async_remote_copy(
        src_ref=src,
        dst_ref=dst,
        send_sem=sends.at[where],
        recv_sem=recvs.at[where],
        device_id=device,
        device_id_type=MESH,
    )


def kernel(
    groups, cycle, slots,
    tok, cot, ids, fix, up_in, down_in,
    mixed_out, grad_tok_out, grad_up_out, grad_down_out,
    mixed, grad_tok, grad_up, grad_down, out_sem,
    up_w, down_w, pick, home_scl, snd_tok, snd_scl, vis_tok, vis_scl,
    acc_h, acc_d, acc_hv, acc_dv, act_h, dh_h, act_v, dh_v, out_h, din_h,
    ret_out, ret_din, back_out, back_din,
    up_pair, down_pair, up_pair_in, down_pair_in, up_own, down_own,
    up_x, down_x, up_x_in, down_x_in,
    local_sem, pair_s, pair_r, x_s, x_r, y_s, y_r, f_s, f_r, d_s, d_r, r_s, r_r,
    gp_s, gp_r, gx_s, gx_r,
):
    rows = tok.shape[0]
    width = tok.shape[1]
    part = width // slots
    highs = slots // 2
    group = lax.axis_index("groups")
    place = lax.axis_index("expert")
    me = lax.axis_index("dp")
    high = me // 2
    low = me % 2
    other = 1 - low
    pair = high * 2 + other
    after = lax.rem(place + 1, cycle)
    before = lax.rem(place + cycle - 1, cycle)

    def columns(block):
        return pl.ds(pl.multiple_of(block * part, part), part)

    barrier = pltpu.get_barrier_semaphore()
    peers = [{"dp": pair}, {"expert": after}, {"expert": before}]
    peers += [{"dp": lax.rem(high + k, highs) * 2 + low} for k in range(1, highs)]
    peers += [{"groups": lax.rem(group + q, groups)} for q in range(1, groups)]
    for peer in peers:
        pl.semaphore_signal(barrier, inc=1, device_id=peer, device_id_type=MESH)

    lane = lax.broadcasted_iota(jnp.int32, (rows, rows), 1)
    line = lax.broadcasted_iota(jnp.int32, (rows, rows), 0)
    eye = jnp.where(line == lane, 1.0, 0.0).astype(BF16)
    goes = jnp.where(ids[1:2, :] == after, 1.0, 0.0).astype(F32)
    upper = lax.broadcasted_iota(jnp.int32, (8, rows), 0) == 0
    marks = jnp.where(upper, goes, 1.0 - goes)
    counts = dot(marks.astype(BF16), jnp.where(line <= lane, 1.0, 0.0).astype(BF16))
    slot = lax.broadcasted_iota(jnp.int32, (2 * CAP, rows), 0)
    first = slot < CAP
    wanted = jnp.where(first, slot, slot - CAP).astype(F32) + 1.0
    count = jnp.where(first, counts[0:1, :], counts[1:2, :])
    mark = jnp.where(first, marks[0:1, :], marks[1:2, :])
    pick[...] = jnp.where(count == wanted, mark, 0.0).astype(BF16)
    fixed = fix[...]
    split = jnp.concatenate([fixed // 256, fixed % 256], axis=0).astype(F32).astype(BF16)
    turned = nt_dot(eye, split)
    home_fix = turned[:, 0:1] * 256.0 + turned[:, 2:3]
    side_fix = turned[:, 1:2] * 256.0 + turned[:, 3:4]
    total = home_fix + side_fix
    home_gate = home_fix / total
    side_gate = side_fix / total

    sends = []

    def begin(copy):
        copy.start()
        sends.append(copy)
        return copy

    ways = ((0, after), (1, before))
    order = [(k, h) for k in list(range(1, highs)) + [0] for h in (other, low)]
    order = [lax.rem(high + k, highs) * 2 + h for k, h in order]
    far = 2 * (highs - 1)
    part_half = part // HALVES
    pieces = [(block, m) for m in range(HALVES) for block in order[:far]]
    pieces += [(block, m) for m in range(HALVES) for block in order[far:]]

    picked = pick[...]
    snd_tok[...] = dot(picked, tok[...]).astype(BF16)
    pl.semaphore_wait(barrier, len(peers))

    tok_copies = []
    for way, target in ways:
        span = pl.ds(way * CAP, CAP)
        copy = remote(snd_tok.at[span], vis_tok.at[span], d_s, d_r, (slots * HALVES, way), {"expert": target})
        tok_copies.append(begin(copy))

    weights = ((up_in, up_w), (down_in, down_w))
    local_copies = []
    pair_copies = []
    x_copies = [[], []]
    for w, (own, full) in enumerate(weights):
        half = own.shape[1] // groups
        mine = pl.ds(pl.multiple_of(group * half, half), half)
        for k in range(1, highs):
            copy = remote(
                own.at[0, mine], full.at[me, mine], x_s, x_r, (w, k - 1),
                {"dp": lax.rem(high + k, highs) * 2 + low},
            )
            x_copies[w].append(begin(copy))
        copy = remote(own.at[0], full.at[me], pair_s, pair_r, w, {"dp": pair})
        pair_copies.append(begin(copy))
        copy = pltpu.make_async_copy(own.at[0], full.at[me], local_sem.at[w])
        copy.start()
        local_copies.append(copy)

    wide = cot[...].astype(F32)
    snd_scl[...] = dot(picked, (side_gate * wide).astype(BF16)).astype(BF16)
    scl_copies = []
    for r, (block, m) in enumerate(pieces):
        span = pl.ds(pl.multiple_of(block * part + m * part_half, part_half), part_half)
        for way, target in ways:
            lines = pl.ds(way * CAP, CAP)
            copy = remote(
                snd_scl.at[lines, span], vis_scl.at[lines, span], d_s, d_r, (r, way), {"expert": target}
            )
            scl_copies.append(begin(copy))
    home_scl[...] = (home_gate * wide).astype(BF16)

    def add_up(block, first_one, src, acc):
        term = dot(src[:, columns(block)], up_w[block])
        acc[...] = term if first_one else acc[...] + term

    def add_down(block, first_one, src, acc):
        term = nt_dot(src[:, columns(block)], down_w[block])
        acc[...] = term if first_one else acc[...] + term

    def forward_x(w, k):
        own, full = weights[w]
        came = lax.rem(high + highs - k, highs) * 2 + low
        half = own.shape[1] // groups
        x_copies[w][k - 1].wait_recv()
        piece = full.at[came, pl.ds(pl.multiple_of(group * half, half), half)]
        for q in range(1, groups):
            y_copies[w, k, q] = begin(remote(
                piece, piece, y_s, y_r, (w, k - 1, q - 1), {"groups": lax.rem(group + q, groups)}
            ))
        f_copies[w, k, 0] = begin(remote(piece, piece, f_s, f_r, (w, k - 1, 0), {"dp": pair}))

    def forward_y(w, k):
        own, full = weights[w]
        came = lax.rem(high + highs - k, highs) * 2 + low
        half = own.shape[1] // groups
        for q in range(1, groups):
            y_copies[w, k, q].wait_recv()
            theirs = lax.rem(group + groups - q, groups)
            piece = full.at[came, pl.ds(pl.multiple_of(theirs * half, half), half)]
            f_copies[w, k, q] = begin(remote(piece, piece, f_s, f_r, (w, k - 1, q), {"dp": pair}))

    y_copies = {}
    f_copies = {}
    local_copies[0].wait()
    add_up(me, True, tok, acc_h)
    pair_copies[0].wait_recv()
    add_up(pair, False, tok, acc_h)
    local_copies[1].wait()
    add_down(me, True, home_scl, acc_d)
    for k in range(1, highs):
        forward_x(0, k)
    pair_copies[1].wait_recv()
    add_down(pair, False, home_scl, acc_d)
    for copy in tok_copies:
        copy.wait_recv()
    add_up(me, True, vis_tok, acc_hv)
    add_up(pair, False, vis_tok, acc_hv)
    for k in range(1, highs):
        forward_x(1, k)
    for k in range(1, highs):
        forward_y(0, k)
        came = lax.rem(high + highs - k, highs) * 2 + low
        add_up(came, False, tok, acc_h)
        add_up(came, False, vis_tok, acc_hv)
    for k in range(1, highs):
        for q in range(groups):
            f_copies[0, k, q].wait_recv()
        came = lax.rem(high + highs - k, highs) * 2 + other
        add_up(came, False, tok, acc_h)
        add_up(came, False, vis_tok, acc_hv)

    def activate(acc, act):
        hidden = acc[...]
        act[...] = (hidden * (1.0 / (1.0 + jnp.exp(-hidden)))).astype(BF16)

    def back_through(acc, d_acc, out):
        hidden = acc[...]
        sig = 1.0 / (1.0 + jnp.exp(-hidden))
        out[...] = (d_acc[...] * sig * (1.0 + hidden * (1.0 - sig))).astype(BF16)

    activate(acc_h, act_h)
    activate(acc_hv, act_v)

    def home_block(block, carry):
        span = columns(block)
        out_h[:, span] = dot(act_h[...], down_w[block]).astype(BF16)
        din_h[:, span] = nt_dot(dh_h[...], up_w[block]).astype(BF16)
        return carry

    r_copies = [[], []]

    def returns(array):
        for block in range(slots):
            span = pl.ds(block * part, part)
            if array == 0:
                src, dst = ret_out, back_out
                src[:, span] = dot(act_v[...], down_w[block]).astype(BF16)
            else:
                src, dst = ret_din, back_din
                src[:, span] = nt_dot(dh_v[...], up_w[block]).astype(BF16)
            for way, target in enumerate((before, after)):
                lines = pl.ds(way * CAP, CAP)
                r_copies[array].append(begin(remote(
                    src.at[lines, span], dst.at[lines, span], r_s, r_r, (array, block, way),
                    {"expert": target},
                )))

    hidden_width = act_h.shape[1]

    def up_term(block, m, dst):
        step = min(256, part_half)

        def one(i, carry):
            start = m * part_half + i * step
            span = pl.ds(pl.multiple_of(block * part + start, step), step)
            term = tn_dot(tok[:, span], dh_h[...]) + tn_dot(vis_tok[:, span], dh_v[...])
            dst[pl.ds(pl.multiple_of(start, step), step), :] = term.astype(dst.dtype)
            return carry

        lax.fori_loop(0, part_half // step, one, 0)

    def down_term(block, m, dst):
        step = 256
        span = pl.ds(pl.multiple_of(block * part + m * part_half, part_half), part_half)
        into = pl.ds(m * part_half, part_half)

        def one(i, carry):
            lines = pl.ds(pl.multiple_of(i * step, step), step)
            term = tn_dot(act_h[:, lines], home_scl[:, span]) + tn_dot(act_v[:, lines], vis_scl[:, span])
            dst[lines, into] = term.astype(dst.dtype)
            return carry

        lax.fori_loop(0, hidden_width // step, one, 0)

    def cut(w, k, m):
        span = pl.ds(m * part_half, part_half)
        return (k, span) if w == 0 else (k, slice(None), span)

    terms = (
        (up_term, up_pair, up_pair_in, up_own, up_x, up_x_in, grad_up),
        (down_term, down_pair, down_pair_in, down_own, down_x, down_x_in, grad_down),
    )
    gp_copies = {}
    gx_copies = {}

    def make_terms(w, k, m):
        make, pair_out, pair_in, own = terms[w][:4]
        target = lax.rem(high + k, highs) * 2
        make(target + other, m, pair_out.at[k])
        where = cut(w, k, m)
        gp_copies[w, k, m] = begin(remote(
            pair_out.at[where], pair_in.at[where], gp_s, gp_r, (w, k, m), {"dp": pair}
        ))
        make(target + low, m, own.at[k])

    def send_x(w, k, m):
        pair_in, own, out, into = terms[w][2:6]
        gp_copies[w, k, m].wait_recv()
        where = cut(w, k, m)
        there = cut(w, k - 1, m)
        out[there] = (own[where] + pair_in[where].astype(F32)).astype(BF16)
        gx_copies[w, k, m] = begin(remote(
            out.at[there], into.at[there], gx_s, gx_r, (w, k - 1, m),
            {"dp": lax.rem(high + k, highs) * 2 + low},
        ))

    for m in range(HALVES):
        for copy in scl_copies[2 * far * m : 2 * far * (m + 1)]:
            copy.wait_recv()
        for k in range(1, highs):
            make_terms(1, k, m)
        for k in range(1, highs):
            send_x(1, k, m)
    for k in range(1, highs):
        forward_y(1, k)
    for k in range(1, highs):
        for q in range(groups):
            f_copies[1, k, q].wait_recv()
    returns(0)
    for k in range(1, highs):
        add_down(lax.rem(high + highs - k, highs) * 2 + low, False, home_scl, acc_d)
        add_down(lax.rem(high + highs - k, highs) * 2 + other, False, home_scl, acc_d)
    back_through(acc_h, acc_d, dh_h)
    for r, block in enumerate(order[:far]):
        add_down(block, r == 0, vis_scl, acc_dv)
    for copy in scl_copies[2 * far * HALVES :]:
        copy.wait_recv()
    for block in order[far:]:
        add_down(block, False, vis_scl, acc_dv)
    back_through(acc_hv, acc_dv, dh_v)
    for m in range(HALVES):
        for k in range(1, highs):
            make_terms(0, k, m)
        for k in range(1, highs):
            send_x(0, k, m)
    returns(1)
    for w in (1, 0):
        for m in range(HALVES):
            make_terms(w, 0, m)
    lax.fori_loop(0, slots, home_block, 0)
    for w in (1, 0):
        pair_in, own = terms[w][2:4]
        for m in range(HALVES):
            gp_copies[w, 0, m].wait_recv()
        own[0] = own[0] + pair_in[0].astype(F32)

    stores = []

    def store(src, dst):
        copy = pltpu.make_async_copy(src, dst, out_sem.at[len(stores)])
        copy.start()
        stores.append(copy)

    def finish(w, m):
        own, _, into, result = terms[w][3:7]
        where = cut(w, 0, m)
        whole = own[where]
        for k in range(1, highs):
            gx_copies[w, k, m].wait_recv()
            whole = whole + into[cut(w, k - 1, m)].astype(F32)
        result[where] = whole.astype(BF16)
        store(result.at[where], (grad_up_out, grad_down_out)[w].at[where])

    picked = pick[...]

    def combine(array, block):
        for copy in r_copies[array][2 * block : 2 * block + 2]:
            copy.wait_recv()
        span = pl.ds(block * part, part)
        if array == 0:
            side = tn_dot(picked, back_out[:, span])
            value = home_gate * out_h[:, span].astype(F32) + side_gate * side
            mixed[:, span] = value.astype(BF16)
        else:
            side = tn_dot(picked, back_din[:, span])
            grad_tok[:, span] = (din_h[:, span].astype(F32) + side).astype(BF16)

    for block in range(slots):
        combine(0, block)
    store(mixed, mixed_out)
    for m in range(HALVES):
        finish(1, m)
    for m in range(HALVES - 1):
        finish(0, m)
    for block in range(slots):
        combine(1, block)
    store(grad_tok, grad_tok_out)
    finish(0, HALVES - 1)
    for copy in stores:
        copy.wait()
    for copy in sends:
        copy.wait_send()


def hand_over(*refs):
    count = (len(refs) - 2) // 3
    sems, done = refs[-2:]
    loads, stores = [], []

    def piece(ref, j):
        middle = ref.shape[-2] // 2
        span = pl.ds(j * middle, middle)
        return ref.at[0, span] if len(ref.shape) == 3 else ref.at[span]

    for i in range(count):
        for j in range(2):
            copy = pltpu.make_async_copy(piece(refs[i], j), piece(refs[2 * count + i], j), sems.at[i, j])
            copy.start()
            loads.append(copy)
    for i in range(count):
        for j in range(2):
            loads[2 * i + j].wait()
            copy = pltpu.make_async_copy(
                piece(refs[2 * count + i], j), piece(refs[count + i], j), done.at[i, j]
            )
            copy.start()
            stores.append(copy)
    for copy in stores:
        copy.wait()


def local(tokens, cotangent, expert_ids, gate_fix, w_up, w_down):
    rows, width = tokens.shape
    groups = lax.axis_size("groups")
    cycle = lax.axis_size("expert")
    slots = lax.axis_size("dp")
    highs = slots // 2
    hidden = w_up.shape[2]
    part = width // slots
    side = 2 * CAP
    vmem = pl.BlockSpec(memory_space=pltpu.VMEM)
    anywhere = pl.BlockSpec(memory_space=pl.ANY)
    dma = pltpu.SemaphoreType.DMA
    far = highs - 1
    results = (
        jax.ShapeDtypeStruct((rows, width), BF16),
        jax.ShapeDtypeStruct((rows, width), BF16),
        jax.ShapeDtypeStruct((1, part, hidden), BF16),
        jax.ShapeDtypeStruct((1, hidden, part), BF16),
    )
    made = pl.pallas_call(
        functools.partial(kernel, groups, cycle, slots),
        out_shape=results,
        in_specs=[vmem] * 4 + [anywhere] * 2,
        out_specs=[anywhere] * 4,
        scratch_shapes=[
            pltpu.VMEM((rows, width), BF16),
            pltpu.VMEM((rows, width), BF16),
            pltpu.VMEM((1, part, hidden), BF16),
            pltpu.VMEM((1, hidden, part), BF16),
            dma((2 + 2 * HALVES,)),
            pltpu.VMEM((slots, part, hidden), BF16),
            pltpu.VMEM((slots, hidden, part), BF16),
            pltpu.VMEM((side, rows), BF16),
            pltpu.VMEM((rows, width), BF16),
            pltpu.VMEM((side, width), BF16),
            pltpu.VMEM((side, width), BF16),
            pltpu.VMEM((side, width), BF16),
            pltpu.VMEM((side, width), BF16),
            pltpu.VMEM((rows, hidden), F32),
            pltpu.VMEM((rows, hidden), F32),
            pltpu.VMEM((side, hidden), F32),
            pltpu.VMEM((side, hidden), F32),
            pltpu.VMEM((rows, hidden), BF16),
            pltpu.VMEM((rows, hidden), BF16),
            pltpu.VMEM((side, hidden), BF16),
            pltpu.VMEM((side, hidden), BF16),
            pltpu.VMEM((rows, width), BF16),
            pltpu.VMEM((rows, width), BF16),
            pltpu.VMEM((side, width), BF16),
            pltpu.VMEM((side, width), BF16),
            pltpu.VMEM((side, width), BF16),
            pltpu.VMEM((side, width), BF16),
            pltpu.VMEM((highs, part, hidden), BF16),
            pltpu.VMEM((highs, hidden, part), BF16),
            pltpu.VMEM((highs, part, hidden), BF16),
            pltpu.VMEM((highs, hidden, part), BF16),
            pltpu.VMEM((highs, part, hidden), F32),
            pltpu.VMEM((highs, hidden, part), F32),
            pltpu.VMEM((far, part, hidden), BF16),
            pltpu.VMEM((far, hidden, part), BF16),
            pltpu.VMEM((far, part, hidden), BF16),
            pltpu.VMEM((far, hidden, part), BF16),
            dma((2,)),
            dma((2,)),
            dma((2,)),
            dma((2, far)),
            dma((2, far)),
            dma((2, far, groups - 1)),
            dma((2, far, groups - 1)),
            dma((2, far, groups)),
            dma((2, far, groups)),
            dma((slots * HALVES + 1, 2)),
            dma((slots * HALVES + 1, 2)),
            dma((2, slots, 2)),
            dma((2, slots, 2)),
            dma((2, highs, HALVES)),
            dma((2, highs, HALVES)),
            dma((2, far, HALVES)),
            dma((2, far, HALVES)),
        ],
        compiler_params=pltpu.CompilerParams(
            collective_id=0, has_side_effects=True, vmem_limit_bytes=56 * 1024 * 1024
        ),
    )(tokens, cotangent, expert_ids.T, gate_fix.T, w_up, w_down)
    return pl.pallas_call(
        hand_over,
        out_shape=results,
        in_specs=[anywhere] * 4,
        out_specs=[anywhere] * 4,
        scratch_shapes=[pltpu.VMEM(shape.shape, BF16) for shape in results] + [dma((4, 2)), dma((4, 2))],
    )(*made)


def solution(mesh):
    in_specs = (
        P(("groups", "expert", "dp"), None),
        P(("groups", "expert", "dp"), None),
        P(("groups", "expert", "dp"), None),
        P(("groups", "expert", "dp"), None),
        P("expert", "dp", None),
        P("expert", None, "dp"),
    )
    out_specs = (
        P(("groups", "expert", "dp"), None),
        P(("groups", "expert", "dp"), None),
        P(("groups", "expert"), "dp", None),
        P(("groups", "expert"), None, "dp"),
    )
    return jax.shard_map(local, mesh=mesh, in_specs=in_specs, out_specs=out_specs, check_vma=False)
```
